256 devices in a mesh: row: 8 (over y, core), col: 32 (over x, z).
Axes of the slice: x: 4, y: 4, z: 8, core: 2. Of those that a mesh axis runs over, the one named last changes fastest.
Arguments:
- matrix: bfloat16 [24576, 24576], P('row', 'col'), may hold values from -8 to 8
- panels: float32 [2, 24576, 128], P(None, ('col', 'row')), may hold values from -0.0390625 to 0.0390625
Outputs:
- updated: bfloat16 [24576, 24576], P('row', 'col')
The draws below stay inside these ranges and needn't reach their ends.
All inputs are finite; a program needn't handle non-finite values.
Results may differ from the reference program's by a relative error of at most 0.0038.
The reference program's roundings to bfloat16 on the way (of `vb` and `wb`) count: a program that leaves them out, or rounds other values in their place, can miss the bound.
Values may be sent and summed in bfloat16 or wider, within the bound.
A program may use at most 64 MiB of HBM per device.

```python
import jax
import jax.numpy as jnp
from jax import lax

N = 24576
NB = 128
PANELS = 2
N_ROW = 8


def draw_matrix(key, part):
    key = jax.random.fold_in(key, 11)
    base = jax.random.normal(key, (N, N), jnp.float32)
    sym = (base + base.T) * 0.70710677
    return jnp.clip(sym, -8.0, 8.0).astype(jnp.bfloat16)


def steps_of(stream_key, dims, cuts, low, high):
    def one(axis_at, blocks):
        draws = jax.random.uniform(jax.random.fold_in(jax.random.fold_in(stream_key, 6), axis_at), (blocks,), jnp.float32, low / len(cuts), high / len(cuts))
        return jnp.repeat(jnp.exp(draws), dims[axis_at] // blocks).reshape((-1,) + (1,) * (len(dims) - axis_at - 1))

    gain = one(*cuts[0])
    for cut in cuts[1:]:
        gain = gain * one(*cut)
    return gain


def centred(rng, shape, spread, reach, cuts=(), held_as=jnp.bfloat16):
    drawn = spread * jax.random.normal(rng, shape, jnp.float32)
    if cuts:
        drawn = drawn * steps_of(rng, shape, cuts, -0.22, 0.18)
    return jnp.clip(drawn, -reach, reach).astype(held_as)


def setup_inputs(seed: int = 0) -> dict:
    keys = jax.random.split(jax.random.key(seed), 3)
    matrix = draw_matrix(jax.random.fold_in(keys[2], 71), 0)
    panels = centred(keys[1], (PANELS, N, NB), N ** -0.5, 0.0390625, ((1, 256),), jnp.float32)
    return {"matrix": matrix, "panels": panels}


def reflector(gram):
    lower = jnp.linalg.cholesky(gram)
    return jax.scipy.linalg.cho_solve((lower, True), 2.0 * jnp.eye(gram.shape[0], dtype=gram.dtype))

def apply_panel(current, vectors, factor):
    highest = lax.Precision.HIGHEST
    vb = vectors.astype(jnp.bfloat16)
    product = jnp.dot(vb.T.astype(jnp.float32), current.astype(jnp.float32), preferred_element_type=jnp.float32).T
    scaled = jnp.dot(product, factor, precision=highest)
    coupling = jnp.dot(vectors.T, scaled, precision=highest)
    wide = scaled - 0.5 * jnp.dot(vectors, jnp.dot(factor, coupling, precision=highest), precision=highest)
    wb = wide.astype(jnp.bfloat16)
    left = jnp.concatenate([vb, wb], axis=1)
    right = jnp.concatenate([wb, vb], axis=1)
    blocks = current.reshape(N_ROW, N // N_ROW, N)
    left_blocks = left.reshape(N_ROW, N // N_ROW, 2 * NB)

    def one_block(pair):
        rows, lhs = pair
        return (rows.astype(jnp.float32) - jnp.dot(lhs.astype(jnp.float32), right.T.astype(jnp.float32), preferred_element_type=jnp.float32)).astype(jnp.bfloat16)
    return lax.map(one_block, (blocks, left_blocks)).reshape(N, N)

def reference(matrix, panels):
    highest = lax.Precision.HIGHEST
    first = panels[0]
    raw_second = panels[1]
    gram_one = jnp.dot(first.T, first, precision=highest)
    cross = jnp.dot(first.T, raw_second, precision=highest)
    factor_one = reflector(gram_one)
    mixing = jnp.dot(factor_one, cross, precision=highest)
    second = raw_second - jnp.dot(first, mixing, precision=highest)
    factor_two = reflector(jnp.dot(second.T, second, precision=highest))
    current = apply_panel(matrix, first, factor_one)
    current = apply_panel(current, second, factor_two)
    return current
```

```python
import functools

import jax
import jax.numpy as jnp
from jax import lax
from jax.experimental import pallas as pl
from jax.experimental.pallas import tpu as pltpu
from jax.sharding import PartitionSpec as P

NB = 128
PIECE = 96
BLOCK = 768
ROWS = 3072
F32 = jnp.float32
BF16 = jnp.bfloat16


def fdot(left, right, contract=((1,), (0,))):
    return lax.dot_general(
        left, right, (contract, ((), ())), precision=lax.Precision.HIGHEST, preferred_element_type=F32
    )


def rcopy(src, dst, send, recv, row, col):
    return pltpu.make_async_remote_copy(
        src_ref=src, dst_ref=dst, send_sem=send, recv_sem=recv,
        device_id=(row, col), device_id_type=pl.DeviceIdType.MESH,
    )


class Where:
    def __init__(self):
        self.r = lax.axis_index("row")
        self.c = lax.axis_index("col")
        self.y = self.r // 2
        self.k = self.r % 2
        self.x = self.c // 8
        self.z = self.c % 8


def loop(lo, hi, body):
    def step(i, carry):
        body(i)
        return carry
    lax.fori_loop(lo, hi, step, 0)


class AllReduce:
    def __init__(self, w, src, refs):
        self.w = w
        self.src = src
        (self.in1, self.acc, self.in2, self.in3, self.g4, self.out,
         self.s1, self.q1, self.s2, self.q2, self.s3, self.q3, self.s4, self.q4, self.s5, self.q5) = refs

    def copy1(self, d):
        w = self.w
        to = (w.r + d) % 8
        return rcopy(self.src.at[pl.ds(pl.multiple_of(to * 64, 64), 64)], self.in1.at[d - 1],
                     self.s1.at[d - 1], self.q1.at[d - 1], to, w.c)

    def copy2(self, d):
        w = self.w
        to = (w.z + d) % 8
        return rcopy(self.acc.at[pl.ds(pl.multiple_of(to * 8, 8), 8)], self.in2.at[d - 1],
                     self.s2.at[d - 1], self.q2.at[d - 1], w.r, w.x * 8 + to)

    def copy3(self, d):
        w = self.w
        to = (w.x + d) % 4
        return rcopy(self.in3.at[0], self.in3.at[d], self.s3.at[d - 1], self.q3.at[d - 1], w.r, to * 8 + w.z)

    def copy4(self, d, owner):
        w = self.w
        to = (w.z + d) % 8
        part = self.g4.at[pl.ds(pl.multiple_of(owner * 8, 8), 8)]
        return rcopy(part, part, self.s4.at[d - 1], self.q4.at[d - 1], w.r, w.x * 8 + to)

    def copy5(self, d, owner):
        w = self.w
        to = (w.r + d) % 8
        part = self.out.at[pl.ds(pl.multiple_of(owner * 64, 64), 64)]
        return rcopy(part, part, self.s5.at[d - 1], self.q5.at[d - 1], to, w.c)

    def step1(self):
        loop(1, 8, lambda d: self.copy1(d).start())

    def step2(self):
        loop(1, 8, lambda d: self.copy1(d).wait_recv())
        total = self.src[pl.ds(pl.multiple_of(self.w.r * 64, 64), 64)]
        for d in range(7):
            total = total + self.in1[d]
        self.acc[...] = total
        loop(1, 8, lambda d: self.copy2(d).start())

    def step3(self):
        loop(1, 8, lambda d: self.copy2(d).wait_recv())
        total = self.acc[pl.ds(pl.multiple_of(self.w.z * 8, 8), 8)]
        for d in range(7):
            total = total + self.in2[d]
        self.in3[0] = total
        loop(1, 4, lambda d: self.copy3(d).start())

    def step4(self):
        z = self.w.z
        loop(1, 4, lambda d: self.copy3(d).wait_recv())
        total = (self.in3[0] + self.in3[2]) + (self.in3[1] + self.in3[3])
        self.g4[pl.ds(pl.multiple_of(z * 8, 8), 8)] = total
        loop(1, 8, lambda d: self.copy4(d, z).start())

    def step5(self):
        w = self.w
        loop(1, 8, lambda d: self.copy4(d, (w.z - d + 8) % 8).wait_recv())
        self.out[pl.ds(pl.multiple_of(w.r * 64, 64), 64)] = self.g4[...]
        loop(1, 8, lambda d: self.copy5(d, w.r).start())

    def finish(self):
        w = self.w
        loop(1, 8, lambda d: self.copy5(d, (w.r - d + 8) % 8).wait_recv())

    def drain(self):
        w = self.w
        loop(1, 8, lambda d: self.copy1(d).wait_send())
        loop(1, 8, lambda d: self.copy2(d).wait_send())
        loop(1, 4, lambda d: self.copy3(d).wait_send())
        loop(1, 8, lambda d: self.copy4(d, w.z).wait_send())
        loop(1, 8, lambda d: self.copy5(d, w.r).wait_send())


class Gather:
    def __init__(self, w, piece, rows, cols, sems):
        self.w = w
        self.piece = piece
        self.rows = rows
        self.cols = cols
        self.cs, self.cq, self.xs, self.xq, self.zs, self.zq = sems

    def col_copy(self, d, owner):
        w = self.w
        return rcopy(self.piece, self.cols.at[pl.ds(pl.multiple_of(owner * PIECE, PIECE), PIECE)],
                     self.cs.at[d - 1], self.cq.at[d - 1], (w.r + d) % 8, w.c)

    def x_copy(self, d, owner):
        w = self.w
        at = pl.multiple_of((w.z % 4) * BLOCK + owner * PIECE, PIECE)
        return rcopy(self.piece, self.rows.at[pl.ds(at, PIECE)], self.xs.at[d], self.xq.at[owner],
                     2 * w.x + w.z // 4, ((w.x + d) % 4) * 8 + w.z)

    def z_copy(self, way, t, at_z):
        w = self.w
        src_z = (at_z - t + 8) % 8 if way == 0 else (at_z + t) % 8
        base = (src_z % 4) * BLOCK
        if t < 3:
            part = self.rows.at[pl.ds(pl.multiple_of(base, BLOCK), BLOCK)]
        else:
            half = BLOCK // 2
            part = self.rows.at[pl.ds(pl.multiple_of(base + way * half, half), half)]
        to = (w.z + 1) % 8 if way == 0 else (w.z + 7) % 8
        copy = rcopy(part, part, self.zs.at[way, t], self.zq.at[way, t], w.r, w.x * 8 + to)
        return copy, src_z // 4 == w.k

    def start(self):
        w = self.w
        for d in range(1, 4):
            self.x_copy(d, w.r).start()
        self_target = w.r == 2 * w.x + w.z // 4

        @pl.when(jnp.logical_not(self_target))
        def _():
            self.x_copy(0, w.r).start()

        @pl.when(self_target)
        def _():
            at = pl.multiple_of((w.z % 4) * BLOCK + w.r * PIECE, PIECE)
            self.rows[pl.ds(at, PIECE)] = self.piece[...]

        loop(1, 8, lambda d: self.col_copy(d, w.r).start())
        self.cols[pl.ds(pl.multiple_of(w.r * PIECE, PIECE), PIECE)] = self.piece[...]

    def wait_x(self):
        w = self.w

        @pl.when(w.z // 4 == w.k)
        def _():
            def one(owner):
                @pl.when(jnp.logical_not(jnp.logical_and(owner == w.r, w.x == w.y)))
                def _():
                    self.x_copy(0, owner).wait_recv()
            loop(0, 8, one)

    def send_z(self, t):
        for way in range(2):
            copy, mine = self.z_copy(way, t, self.w.z)

            @pl.when(mine)
            def _():
                copy.start()

    def wait_z(self, t):
        z = self.w.z
        for way in range(2):
            copy, mine = self.z_copy(way, t, (z + 7) % 8 if way == 0 else (z + 1) % 8)

            @pl.when(mine)
            def _():
                copy.wait_recv()

    def step(self, t):
        if t == 0:
            self.wait_x()
        else:
            self.wait_z(t - 1)
        if t < 4:
            self.send_z(t)

    def wait_cols(self):
        w = self.w
        loop(1, 8, lambda d: self.col_copy(d, (w.r - d + 8) % 8).wait_recv())

    def drain(self):
        w = self.w
        for d in range(1, 4):
            self.x_copy(d, w.r).wait_send()

        @pl.when(w.r != 2 * w.x + w.z // 4)
        def _():
            self.x_copy(0, w.r).wait_send()

        loop(1, 8, lambda d: self.col_copy(d, w.r).wait_send())
        for t in range(4):
            for way in range(2):
                copy, mine = self.z_copy(way, t, w.z)

                @pl.when(mine)
                def _():
                    copy.wait_send()


def invert(work, lo, hi):
    sub = lax.broadcasted_iota(jnp.int32, (8, 2 * NB), 0)

    def panel(p):
        at = pl.multiple_of(p * 8, 8)
        for m in range(2):
            rows = work[m, pl.ds(at, 8), :]
            for j in range(8):
                pivot = rows[j:j + 1, :] / rows[j:j + 1, j:j + 1]
                rows = jnp.where(sub == j, pivot, rows - rows[:, j:j + 1] * pivot)
            whole = work[m]
            new = whole
            for j in range(8):
                new = new - whole[:, j:j + 1] * rows[j:j + 1, :]
            work[m, :, 0:NB] = pltpu.roll(new[:, :NB], NB - 8, 1)
            work[m, :, NB:] = new[:, NB:]
            work[m, pl.ds(at, 8), 0:NB] = pltpu.roll(rows[:, :NB], NB - 8, 1)
            work[m, pl.ds(at, 8), NB:] = rows[:, NB:]
    loop(lo, hi, panel)


def kernel(a_hbm, pan, out, a, piece_x, piece_v, piece_w, rows_x, rows_v, rows_w, cols_x, cols_v, cols_w,
           gram, inner, yt, y, y_in, work, load_sem, store_sem, ys, yq, *rest):
    w = Where()
    n_ar = 16
    ar_g = AllReduce(w, gram, rest[:n_ar])
    ar_s = AllReduce(w, inner, rest[n_ar:2 * n_ar])
    sems = rest[2 * n_ar:]
    g_x = Gather(w, piece_x, rows_x, cols_x, sems[0:6])
    g_v = Gather(w, piece_v, rows_v, cols_v, sems[6:12])
    g_w = Gather(w, piece_w, rows_w, cols_w, sems[12:18])

    load = pltpu.make_async_copy(a_hbm, a, load_sem)
    load.start()
    v1 = pan[0]
    p2 = pan[1]
    piece_x[:, 0:NB] = v1.astype(BF16)
    piece_x[:, NB:] = p2.astype(BF16)
    g_x.start()
    both = jnp.concatenate([v1, p2], axis=1)
    gram[0:256] = fdot(both, v1, ((0,), (0,)))
    gram[256:512] = fdot(both, p2, ((0,), (0,)))
    ar_g.step1()
    g_x.step(0)
    ar_g.step2()
    g_x.step(1)
    ar_g.step3()
    g_x.step(2)
    ar_g.step4()
    g_x.step(3)
    ar_g.step5()
    g_x.step(4)
    load.wait()

    yt[...] = jnp.zeros_like(yt)

    def product(i):
        at = pl.ds(pl.multiple_of(i * 256, 256), 256)
        yt[...] += lax.dot_general(rows_x[at], a[at], (((0,), (0,)), ((), ())), preferred_element_type=F32)
    loop(0, ROWS // 256, product)
    y[...] = yt[...].T
    g_x.wait_cols()

    def y_copy(d):
        to = (w.r + d) % 8
        return rcopy(y.at[pl.ds(pl.multiple_of(to * PIECE, PIECE), PIECE)], y_in.at[d - 1],
                     ys.at[d - 1], yq.at[d - 1], to, w.c)

    hi = yt[...].astype(BF16)
    lo = (yt[...] - hi.astype(F32)).astype(BF16)
    s_t = (lax.dot_general(hi, cols_x[...], (((1,), (0,)), ((), ())), preferred_element_type=F32)
           + lax.dot_general(lo, cols_x[...], (((1,), (0,)), ((), ())), preferred_element_type=F32))
    inner[0:256] = s_t[:, 0:NB]
    inner[256:512] = s_t[:, NB:]
    ar_s.step1()
    loop(1, 8, lambda d: y_copy(d).start())

    ar_g.finish()
    g1 = ar_g.out[0:128]
    cross = ar_g.out[256:384]
    g2 = ar_g.out[384:512]
    eye2 = jnp.where(lax.broadcasted_iota(jnp.int32, (NB, NB), 0) == lax.broadcasted_iota(jnp.int32, (NB, NB), 1),
                     2.0, 0.0).astype(F32)
    work[0, :, 0:NB] = g1
    work[1, :, 0:NB] = g2
    work[0, :, NB:] = eye2
    work[1, :, NB:] = eye2
    invert(work, 0, 4)
    ar_s.step2()
    invert(work, 4, 8)
    ar_s.step3()
    invert(work, 8, 12)
    ar_s.step4()
    invert(work, 12, 16)
    ar_s.step5()
    f1 = work[0, :, NB:]
    f2 = work[1, :, NB:]
    mix = fdot(f1, cross)
    v2 = p2 - fdot(v1, mix)
    piece_v[...] = v2.astype(BF16)
    g_v.start()

    loop(1, 8, lambda d: y_copy(d).wait_recv())
    total = y[pl.ds(pl.multiple_of(w.r * PIECE, PIECE), PIECE)]
    for d in range(7):
        total = total + y_in[d]
    y1 = total[:, 0:NB]
    y2 = total[:, NB:] - fdot(y1, mix)
    ar_s.finish()
    g_v.step(0)
    s11 = ar_s.out[0:128]
    s21 = ar_s.out[128:256]
    s12 = ar_s.out[256:384]
    s22 = ar_s.out[384:512]
    tt = (((0,), (0,)))
    b12 = s12 - fdot(s11, mix)
    b21 = s21 - fdot(mix, s11, tt)
    b22 = s22 - fdot(s21, mix) - fdot(mix, b12, tt)
    k1 = fdot(s11, f1, tt)
    l1 = 0.5 * fdot(f1, k1)
    g_v.step(1)
    h = fdot(f1, b12, tt) + fdot(l1, cross, tt)
    hc = fdot(h, cross, tt)
    k2 = fdot(b22.T + hc + hc.T, f2)
    l2 = 0.5 * fdot(f2, k2)
    w1 = fdot(y1, f1) - fdot(v1, l1)
    prod2 = y2 + fdot(w1, cross) - fdot(v1, h)
    w2 = fdot(prod2, f2) - fdot(v2, l2)
    piece_w[:, 0:NB] = w1.astype(BF16)
    piece_w[:, NB:] = w2.astype(BF16)
    g_w.start()
    g_v.step(2)
    g_w.step(0)
    g_v.step(3)
    g_w.step(1)
    g_v.step(4)
    g_w.step(2)
    g_w.step(3)
    g_w.step(4)
    g_v.wait_cols()
    g_w.wait_cols()

    def store(i):
        at = pl.ds(pl.multiple_of(i * 256, 256), 256)
        return pltpu.make_async_copy(a.at[at], out.at[at], store_sem.at[i])

    right1 = jnp.concatenate([cols_w[:, 0:NB], cols_x[:, 0:NB]], axis=1)
    right2 = jnp.concatenate([cols_w[:, NB:], cols_v[...]], axis=1)

    def update(i):
        at = pl.ds(pl.multiple_of(i * 256, 256), 256)
        nt = (((1,), (1,)), ((), ()))
        left1 = jnp.concatenate([rows_x[at, 0:NB], rows_w[at, 0:NB]], axis=1)
        left2 = jnp.concatenate([rows_v[at, :], rows_w[at, NB:]], axis=1)
        one = (a[at].astype(F32) - lax.dot_general(left1, right1, nt, preferred_element_type=F32)).astype(BF16)
        two = one.astype(F32) - lax.dot_general(left2, right2, nt, preferred_element_type=F32)
        a[at] = two.astype(BF16)
        store(i).start()
    loop(0, ROWS // 256, update)

    ar_g.drain()
    ar_s.drain()
    g_x.drain()
    g_v.drain()
    g_w.drain()
    loop(1, 8, lambda d: y_copy(d).wait_send())
    loop(0, ROWS // 256, lambda i: store(i).wait())


def scratch():
    vm = pltpu.VMEM
    dma = pltpu.SemaphoreType.DMA
    shapes = [
        vm((ROWS, BLOCK), BF16),
        vm((PIECE, 256), BF16), vm((PIECE, 128), BF16), vm((PIECE, 256), BF16),
        vm((ROWS, 256), BF16), vm((ROWS, 128), BF16), vm((ROWS, 256), BF16),
        vm((BLOCK, 256), BF16), vm((BLOCK, 128), BF16), vm((BLOCK, 256), BF16),
        vm((512, 128), F32), vm((512, 128), F32),
        vm((256, BLOCK), F32), vm((BLOCK, 256), F32), vm((7, PIECE, 256), F32),
        vm((2, NB, 2 * NB), F32),
        dma(()), dma((ROWS // 256,)), dma((7,)), dma((7,)),
    ]
    for _ in range(2):
        shapes += [
            vm((7, 64, 128), F32), vm((64, 128), F32), vm((7, 8, 128), F32), vm((4, 8, 128), F32),
            vm((64, 128), F32), vm((512, 128), F32),
            dma((7,)), dma((7,)), dma((7,)), dma((7,)), dma((3,)), dma((3,)), dma((7,)), dma((7,)), dma((7,)), dma((7,)),
        ]
    for _ in range(3):
        shapes += [dma((7,)), dma((7,)), dma((4,)), dma((8,)), dma((2, 4)), dma((2, 4))]
    return shapes


def per_device(matrix, panels):
    return pl.pallas_call(
        kernel,
        out_shape=jax.ShapeDtypeStruct((ROWS, BLOCK), BF16),
        in_specs=[pl.BlockSpec(memory_space=pl.ANY), pl.BlockSpec(memory_space=pltpu.VMEM)],
        out_specs=pl.BlockSpec(memory_space=pl.ANY),
        scratch_shapes=scratch(),
        compiler_params=pltpu.CompilerParams(has_side_effects=True, vmem_limit_bytes=48 * 1024 * 1024),
        cost_estimate=pl.CostEstimate(flops=3700000000, bytes_accessed=9437184, transcendentals=0),
    )(matrix, panels)


def solution(mesh):
    placed = (P("row", "col"), P(None, ("col", "row"), None))
    return jax.shard_map(
        per_device, mesh=mesh, in_specs=placed, out_specs=P("row", "col"), check_vma=False
    )
```

```python
import functools

import jax
import jax.numpy as jnp
from jax import lax
from jax.experimental import pallas as pl
from jax.experimental.pallas import tpu as pltpu
from jax.sharding import PartitionSpec as P

NB = 128
PIECE = 96
BLOCK = 768
ROWS = 3072
F32 = jnp.float32
BF16 = jnp.bfloat16


def fdot(left, right, contract=((1,), (0,))):
    return lax.dot_general(
        left, right, (contract, ((), ())), precision=lax.Precision.HIGHEST, preferred_element_type=F32
    )


def rcopy(src, dst, send, recv, row, col):
    return pltpu.make_async_remote_copy(
        src_ref=src, dst_ref=dst, send_sem=send, recv_sem=recv,
        device_id=(row, col), device_id_type=pl.DeviceIdType.MESH,
    )


class Where:
    def __init__(self):
        self.r = lax.axis_index("row")
        self.c = lax.axis_index("col")
        self.y = self.r // 2
        self.k = self.r % 2
        self.x = self.c // 8
        self.z = self.c % 8


def loop(lo, hi, body):
    def step(i, carry):
        body(i)
        return carry
    lax.fori_loop(lo, hi, step, 0)


class AllReduce:
    def __init__(self, w, src, refs):
        self.w = w
        self.src = src
        (self.in1, self.acc, self.in2, self.in3, self.g4, self.out,
         self.s1, self.q1, self.s2, self.q2, self.s3, self.q3, self.s4, self.q4, self.s5, self.q5) = refs

    def copy1(self, d):
        w = self.w
        to = (w.r + d) % 8
        return rcopy(self.src.at[pl.ds(pl.multiple_of(to * 64, 64), 64)], self.in1.at[d - 1],
                     self.s1.at[d - 1], self.q1.at[d - 1], to, w.c)

    def copy2(self, d):
        w = self.w
        to = (w.z + d) % 8
        return rcopy(self.acc.at[pl.ds(pl.multiple_of(to * 8, 8), 8)], self.in2.at[d - 1],
                     self.s2.at[d - 1], self.q2.at[d - 1], w.r, w.x * 8 + to)

    def copy3(self, d):
        w = self.w
        to = (w.x + d) % 4
        return rcopy(self.in3.at[0], self.in3.at[d], self.s3.at[d - 1], self.q3.at[d - 1], w.r, to * 8 + w.z)

    def copy4(self, d, owner):
        w = self.w
        to = (w.z + d) % 8
        part = self.g4.at[pl.ds(pl.multiple_of(owner * 8, 8), 8)]
        return rcopy(part, part, self.s4.at[d - 1], self.q4.at[d - 1], w.r, w.x * 8 + to)

    def copy5(self, d, owner):
        w = self.w
        to = (w.r + d) % 8
        part = self.out.at[pl.ds(pl.multiple_of(owner * 64, 64), 64)]
        return rcopy(part, part, self.s5.at[d - 1], self.q5.at[d - 1], to, w.c)

    def step1(self):
        loop(1, 8, lambda d: self.copy1(d).start())

    def step2(self):
        loop(1, 8, lambda d: self.copy1(d).wait_recv())
        total = self.src[pl.ds(pl.multiple_of(self.w.r * 64, 64), 64)]
        for d in range(7):
            total = total + self.in1[d]
        self.acc[...] = total
        loop(1, 8, lambda d: self.copy2(d).start())

    def step3(self):
        loop(1, 8, lambda d: self.copy2(d).wait_recv())
        total = self.acc[pl.ds(pl.multiple_of(self.w.z * 8, 8), 8)]
        for d in range(7):
            total = total + self.in2[d]
        self.in3[0] = total
        loop(1, 4, lambda d: self.copy3(d).start())

    def step4(self):
        z = self.w.z
        loop(1, 4, lambda d: self.copy3(d).wait_recv())
        total = (self.in3[0] + self.in3[2]) + (self.in3[1] + self.in3[3])
        self.g4[pl.ds(pl.multiple_of(z * 8, 8), 8)] = total
        loop(1, 8, lambda d: self.copy4(d, z).start())

    def step5(self):
        w = self.w
        loop(1, 8, lambda d: self.copy4(d, (w.z - d + 8) % 8).wait_recv())
        self.out[pl.ds(pl.multiple_of(w.r * 64, 64), 64)] = self.g4[...]
        loop(1, 8, lambda d: self.copy5(d, w.r).start())

    def finish(self):
        w = self.w
        loop(1, 8, lambda d: self.copy5(d, (w.r - d + 8) % 8).wait_recv())

    def drain(self):
        w = self.w
        loop(1, 8, lambda d: self.copy1(d).wait_send())
        loop(1, 8, lambda d: self.copy2(d).wait_send())
        loop(1, 4, lambda d: self.copy3(d).wait_send())
        loop(1, 8, lambda d: self.copy4(d, w.z).wait_send())
        loop(1, 8, lambda d: self.copy5(d, w.r).wait_send())


class Gather:
    def __init__(self, w, piece, rows, cols, sems):
        self.w = w
        self.piece = piece
        self.rows = rows
        self.cols = cols
        self.cs, self.cq, self.xs, self.xq, self.zs, self.zq = sems

    def col_copy(self, d, owner):
        w = self.w
        return rcopy(self.piece, self.cols.at[pl.ds(pl.multiple_of(owner * PIECE, PIECE), PIECE)],
                     self.cs.at[d - 1], self.cq.at[d - 1], (w.r + d) % 8, w.c)

    def x_copy(self, d, owner):
        w = self.w
        at = pl.multiple_of((w.z % 4) * BLOCK + owner * PIECE, PIECE)
        return rcopy(self.piece, self.rows.at[pl.ds(at, PIECE)], self.xs.at[d], self.xq.at[owner],
                     2 * w.x + w.z // 4, ((w.x + d) % 4) * 8 + w.z)

    def z_copy(self, way, t, at_z):
        w = self.w
        src_z = (at_z - t + 8) % 8 if way == 0 else (at_z + t) % 8
        base = (src_z % 4) * BLOCK
        if t < 3:
            part = self.rows.at[pl.ds(pl.multiple_of(base, BLOCK), BLOCK)]
        else:
            half = BLOCK // 2
            part = self.rows.at[pl.ds(pl.multiple_of(base + way * half, half), half)]
        to = (w.z + 1) % 8 if way == 0 else (w.z + 7) % 8
        copy = rcopy(part, part, self.zs.at[way, t], self.zq.at[way, t], w.r, w.x * 8 + to)
        return copy, src_z // 4 == w.k

    def start(self):
        w = self.w
        for d in range(1, 4):
            self.x_copy(d, w.r).start()
        self_target = w.r == 2 * w.x + w.z // 4

        @pl.when(jnp.logical_not(self_target))
        def _():
            self.x_copy(0, w.r).start()

        @pl.when(self_target)
        def _():
            at = pl.multiple_of((w.z % 4) * BLOCK + w.r * PIECE, PIECE)
            self.rows[pl.ds(at, PIECE)] = self.piece[...]

        loop(1, 8, lambda d: self.col_copy(d, w.r).start())
        self.cols[pl.ds(pl.multiple_of(w.r * PIECE, PIECE), PIECE)] = self.piece[...]

    def wait_x(self):
        w = self.w

        @pl.when(w.z // 4 == w.k)
        def _():
            def one(owner):
                @pl.when(jnp.logical_not(jnp.logical_and(owner == w.r, w.x == w.y)))
                def _():
                    self.x_copy(0, owner).wait_recv()
            loop(0, 8, one)

    def send_z(self, t):
        for way in range(2):
            copy, mine = self.z_copy(way, t, self.w.z)

            @pl.when(mine)
            def _():
                copy.start()

    def wait_z(self, t):
        z = self.w.z
        for way in range(2):
            copy, mine = self.z_copy(way, t, (z + 7) % 8 if way == 0 else (z + 1) % 8)

            @pl.when(mine)
            def _():
                copy.wait_recv()

    def step(self, t):
        if t == 0:
            self.wait_x()
        else:
            self.wait_z(t - 1)
        if t < 4:
            self.send_z(t)

    def wait_cols(self):
        w = self.w
        loop(1, 8, lambda d: self.col_copy(d, (w.r - d + 8) % 8).wait_recv())

    def drain(self):
        w = self.w
        for d in range(1, 4):
            self.x_copy(d, w.r).wait_send()

        @pl.when(w.r != 2 * w.x + w.z // 4)
        def _():
            self.x_copy(0, w.r).wait_send()

        loop(1, 8, lambda d: self.col_copy(d, w.r).wait_send())
        for t in range(4):
            for way in range(2):
                copy, mine = self.z_copy(way, t, w.z)

                @pl.when(mine)
                def _():
                    copy.wait_send()


def invert(work, lo, hi):
    sub = lax.broadcasted_iota(jnp.int32, (8, 2 * NB), 0)

    def panel(p):
        at = pl.multiple_of(p * 8, 8)
        for m in range(2):
            rows = work[m, pl.ds(at, 8), :]
            for j in range(8):
                pivot = rows[j:j + 1, :] / rows[j:j + 1, j:j + 1]
                rows = jnp.where(sub == j, pivot, rows - rows[:, j:j + 1] * pivot)
            whole = work[m]
            new = whole
            for j in range(8):
                new = new - whole[:, j:j + 1] * rows[j:j + 1, :]
            work[m, :, 0:NB] = pltpu.roll(new[:, :NB], NB - 8, 1)
            work[m, :, NB:] = new[:, NB:]
            work[m, pl.ds(at, 8), 0:NB] = pltpu.roll(rows[:, :NB], NB - 8, 1)
            work[m, pl.ds(at, 8), NB:] = rows[:, NB:]
    loop(lo, hi, panel)


def barrier(w):
    sem = pltpu.get_barrier_semaphore()

    def greet(row, col):
        pl.semaphore_signal(sem, inc=1, device_id=(row, col), device_id_type=pl.DeviceIdType.MESH)

    loop(1, 8, lambda d: greet((w.r + d) % 8, w.c))
    loop(1, 8, lambda d: greet(w.r, w.x * 8 + (w.z + d) % 8))
    loop(1, 4, lambda d: greet(w.r, (w.x + d) % 4 * 8 + w.z))
    target = 2 * w.x + w.z // 4
    loop(1, 4, lambda d: greet(target, (w.x + d) % 4 * 8 + w.z))
    outside = w.r != target

    @pl.when(outside)
    def _():
        greet(target, w.c)

    receives = w.z // 4 == w.k

    @pl.when(receives)
    def _():
        def one(owner):
            @pl.when(jnp.logical_not(jnp.logical_and(owner == w.r, w.x == w.y)))
            def _():
                greet(owner, 8 * w.y + w.z)
        loop(0, 8, one)

    count = 20 + jnp.where(outside, 1, 0) + jnp.where(receives, jnp.where(w.x == w.y, 7, 8), 0)
    pl.semaphore_wait(sem, count)


def split(value):
    hi = value.astype(BF16)
    return hi, (value - hi.astype(F32)).astype(BF16)


def bdot(left, right, contract=((1,), (0,))):
    return lax.dot_general(left, right, (contract, ((), ())), preferred_element_type=F32)


def kernel(a_hbm, pan, out, a, piece_x, piece_y, rows_x, rows_y, cols_x, cols_y,
           gram, inner, yt, y, y_in, work, coef, right1, right2, load_sem, store_sem, ys, yq, *rest):
    w = Where()
    n_ar = 16
    ar_g = AllReduce(w, gram, rest[:n_ar])
    ar_s = AllReduce(w, inner, rest[n_ar:2 * n_ar])
    sems = rest[2 * n_ar:]
    g_x = Gather(w, piece_x, rows_x, cols_x, sems[0:6])
    g_y = Gather(w, piece_y, rows_y, cols_y, sems[6:12])

    load = pltpu.make_async_copy(a_hbm, a, load_sem)
    load.start()
    v1 = pan[0]
    p2 = pan[1]
    piece_x[:, 0:NB] = v1.astype(BF16)
    piece_x[:, NB:] = p2.astype(BF16)
    barrier(w)
    g_x.start()
    both = jnp.concatenate([v1, p2], axis=1)
    gram[0:256] = fdot(both, v1, ((0,), (0,)))
    gram[256:512] = fdot(both, p2, ((0,), (0,)))
    ar_g.step1()
    yt[...] = jnp.zeros_like(yt)

    def product_block(b):
        def tile(i):
            at = pl.ds(pl.multiple_of(b * BLOCK + i * 256, 256), 256)
            yt[...] += bdot(rows_x[at], a[at], ((0,), (0,)))
        loop(0, BLOCK // 256, tile)

    def product(t):
        for way in range(2 if 0 < t < 4 else 1):
            src_z = (w.z - t + 8) % 8 if way == 0 else (w.z + t) % 8

            @pl.when(src_z // 4 == w.k)
            def _():
                product_block(src_z % 4)

    g_x.step(0)
    ar_g.step2()
    load.wait()
    product(0)
    g_x.step(1)
    ar_g.step3()
    product(1)
    g_x.step(2)
    ar_g.step4()
    product(2)
    g_x.step(3)
    ar_g.step5()
    product(3)
    g_x.step(4)
    product(4)
    y[...] = yt[...].T

    def y_copy(d):
        to = (w.r + d) % 8
        return rcopy(y.at[pl.ds(pl.multiple_of(to * PIECE, PIECE), PIECE)], y_in.at[d - 1],
                     ys.at[d - 1], yq.at[d - 1], to, w.c)

    loop(1, 8, lambda d: y_copy(d).start())
    g_x.wait_cols()
    hi, lo = split(yt[...])
    s_t = bdot(hi, cols_x[...]) + bdot(lo, cols_x[...])
    inner[0:256] = s_t[:, 0:NB]
    inner[256:512] = s_t[:, NB:]
    ar_s.step1()

    ar_g.finish()
    cross = ar_g.out[256:384]
    eye2 = jnp.where(lax.broadcasted_iota(jnp.int32, (NB, NB), 0) == lax.broadcasted_iota(jnp.int32, (NB, NB), 1),
                     2.0, 0.0).astype(F32)
    work[0, :, 0:NB] = ar_g.out[0:128]
    work[1, :, 0:NB] = ar_g.out[384:512]
    work[0, :, NB:] = eye2
    work[1, :, NB:] = eye2
    invert(work, 0, 6)
    ar_s.step2()
    invert(work, 6, 12)
    ar_s.step3()
    loop(1, 8, lambda d: y_copy(d).wait_recv())
    total = y[pl.ds(pl.multiple_of(w.r * PIECE, PIECE), PIECE)]
    for d in range(7):
        total = total + y_in[d]
    piece_y[...] = total.astype(BF16)
    g_y.start()
    invert(work, 12, 16)
    ar_s.step4()
    g_y.step(0)
    f1 = work[0, :, NB:]
    f2 = work[1, :, NB:]
    mix = fdot(f1, cross)
    mix2 = fdot(cross, f2)
    ar_s.step5()
    g_y.step(1)
    ar_s.finish()
    s11 = ar_s.out[0:128]
    s21 = ar_s.out[128:256]
    s12 = ar_s.out[256:384]
    s22 = ar_s.out[384:512]
    tt = ((0,), (0,))
    b12 = s12 - fdot(s11, mix)
    b22 = s22 - fdot(s21, mix) - fdot(mix, b12, tt)
    l1 = 0.5 * fdot(f1, fdot(s11, f1, tt))
    h = fdot(f1, b12, tt) + fdot(l1, cross, tt)
    g_y.step(2)
    hc = fdot(h, cross, tt)
    l2 = 0.5 * fdot(f2, fdot(b22.T + hc + hc.T, f2))
    b = fdot(mix, l2) - (fdot(l1, mix2) + fdot(h, f2))
    for n, part in enumerate((f1, -l1, f2, b, -l2, -mix)):
        hi, lo = split(part)
        coef[n, 0] = hi
        coef[n, 1] = lo
    g_y.step(3)
    g_y.step(4)
    g_y.wait_cols()

    def times(left, n):
        return bdot(left, coef[n, 0]) + bdot(left, coef[n, 1])

    def form(x_ref, y_ref, at):
        v1b = x_ref[at, 0:NB]
        p2b = x_ref[at, NB:]
        w1 = times(y_ref[at, 0:NB], 0) + times(v1b, 1)
        w2 = times(y_ref[at, NB:], 2) + times(v1b, 3) + times(p2b, 4)
        v2 = p2b.astype(F32) + times(v1b, 5)
        return v1b, w1.astype(BF16), v2.astype(BF16), w2.astype(BF16)

    def right(i):
        at = pl.ds(pl.multiple_of(i * 256, 256), 256)
        v1b, w1, v2, w2 = form(cols_x, cols_y, at)
        right1[at, 0:NB] = w1
        right1[at, NB:] = v1b
        right2[at, 0:NB] = w2
        right2[at, NB:] = v2
    loop(0, BLOCK // 256, right)

    def store(i):
        at = pl.ds(pl.multiple_of(i * 256, 256), 256)
        return pltpu.make_async_copy(a.at[at], out.at[at], store_sem.at[i])

    def update(i):
        at = pl.ds(pl.multiple_of(i * 256, 256), 256)
        nt = ((1,), (1,))
        v1b, w1, v2, w2 = form(rows_x, rows_y, at)
        left1 = jnp.concatenate([v1b, w1], axis=1)
        left2 = jnp.concatenate([v2, w2], axis=1)
        one = (a[at].astype(F32) - bdot(left1, right1[...], nt)).astype(BF16)
        a[at] = (one.astype(F32) - bdot(left2, right2[...], nt)).astype(BF16)
        store(i).start()
    loop(0, ROWS // 256, update)

    ar_g.drain()
    ar_s.drain()
    g_x.drain()
    g_y.drain()
    loop(1, 8, lambda d: y_copy(d).wait_send())
    loop(0, ROWS // 256, lambda i: store(i).wait())


def scratch():
    vm = pltpu.VMEM
    dma = pltpu.SemaphoreType.DMA
    shapes = [
        vm((ROWS, BLOCK), BF16),
        vm((PIECE, 256), BF16), vm((PIECE, 256), BF16),
        vm((ROWS, 256), BF16), vm((ROWS, 256), BF16),
        vm((BLOCK, 256), BF16), vm((BLOCK, 256), BF16),
        vm((512, 128), F32), vm((512, 128), F32),
        vm((256, BLOCK), F32), vm((BLOCK, 256), F32), vm((7, PIECE, 256), F32),
        vm((2, NB, 2 * NB), F32),
        vm((6, 2, NB, NB), BF16), vm((BLOCK, 256), BF16), vm((BLOCK, 256), BF16),
        dma(()), dma((ROWS // 256,)), dma((7,)), dma((7,)),
    ]
    for _ in range(2):
        shapes += [
            vm((7, 64, 128), F32), vm((64, 128), F32), vm((7, 8, 128), F32), vm((4, 8, 128), F32),
            vm((64, 128), F32), vm((512, 128), F32),
            dma((7,)), dma((7,)), dma((7,)), dma((7,)), dma((3,)), dma((3,)), dma((7,)), dma((7,)), dma((7,)), dma((7,)),
        ]
    for _ in range(2):
        shapes += [dma((7,)), dma((7,)), dma((4,)), dma((8,)), dma((2, 4)), dma((2, 4))]
    return shapes


def per_device(matrix, panels):
    return pl.pallas_call(
        kernel,
        out_shape=jax.ShapeDtypeStruct((ROWS, BLOCK), BF16),
        in_specs=[pl.BlockSpec(memory_space=pl.ANY), pl.BlockSpec(memory_space=pltpu.VMEM)],
        out_specs=pl.BlockSpec(memory_space=pl.ANY),
        scratch_shapes=scratch(),
        compiler_params=pltpu.CompilerParams(collective_id=0, has_side_effects=True, vmem_limit_bytes=48 * 1024 * 1024),
        cost_estimate=pl.CostEstimate(flops=3700000000, bytes_accessed=9437184, transcendentals=0),
    )(matrix, panels)


def solution(mesh):
    placed = (P("row", "col"), P(None, ("col", "row"), None))
    return jax.shard_map(
        per_device, mesh=mesh, in_specs=placed, out_specs=P("row", "col"), check_vma=False
    )
```

```python
import functools

import jax
import jax.numpy as jnp
from jax import lax
from jax.experimental import pallas as pl
from jax.experimental.pallas import tpu as pltpu
from jax.sharding import PartitionSpec as P

NB = 128
PIECE = 96
BLOCK = 768
ROWS = 3072
F32 = jnp.float32
BF16 = jnp.bfloat16


def fdot(left, right, contract=((1,), (0,))):
    return lax.dot_general(
        left, right, (contract, ((), ())), precision=lax.Precision.HIGHEST, preferred_element_type=F32
    )


def rcopy(src, dst, send, recv, row, col):
    return pltpu.make_async_remote_copy(
        src_ref=src, dst_ref=dst, send_sem=send, recv_sem=recv,
        device_id=(row, col), device_id_type=pl.DeviceIdType.MESH,
    )


class Where:
    def __init__(self):
        self.r = lax.axis_index("row")
        self.c = lax.axis_index("col")
        self.y = self.r // 2
        self.k = self.r % 2
        self.x = self.c // 8
        self.z = self.c % 8


def loop(lo, hi, body):
    def step(i, carry):
        body(i)
        return carry
    lax.fori_loop(lo, hi, step, 0)


class AllReduce:
    def __init__(self, w, src, refs):
        self.w = w
        self.src = src
        (self.in1, self.acc, self.in2, self.in3, self.g4, self.out,
         self.s1, self.q1, self.s2, self.q2, self.s3, self.q3, self.s4, self.q4, self.s5, self.q5) = refs

    def copy1(self, d):
        w = self.w
        to = (w.r + d) % 8
        return rcopy(self.src.at[pl.ds(pl.multiple_of(to * 64, 64), 64)], self.in1.at[d - 1],
                     self.s1.at[d - 1], self.q1.at[d - 1], to, w.c)

    def copy2(self, d):
        w = self.w
        to = (w.x + d) % 4
        return rcopy(self.acc.at[pl.ds(pl.multiple_of(to * 16, 16), 16)], self.in2.at[d - 1],
                     self.s2.at[d - 1], self.q2.at[d - 1], w.r, to * 8 + w.z)

    def copy3(self, d, slot):
        w = self.w
        to = (w.z + d) % 8
        return rcopy(self.in3.at[slot], self.in3.at[slot], self.s3.at[d - 1], self.q3.at[d - 1], w.r, w.x * 8 + to)

    def copy4(self, d, owner):
        w = self.w
        to = (w.x + d) % 4
        part = self.g4.at[pl.ds(pl.multiple_of(owner * 16, 16), 16)]
        return rcopy(part, part, self.s4.at[d - 1], self.q4.at[d - 1], w.r, to * 8 + w.z)

    def copy5(self, d, owner):
        w = self.w
        to = (w.r + d) % 8
        part = self.out.at[pl.ds(pl.multiple_of(owner * 64, 64), 64)]
        return rcopy(part, part, self.s5.at[d - 1], self.q5.at[d - 1], to, w.c)

    def step1(self):
        loop(1, 8, lambda d: self.copy1(d).start())

    def step2(self):
        loop(1, 8, lambda d: self.copy1(d).wait_recv())
        total = self.src[pl.ds(pl.multiple_of(self.w.r * 64, 64), 64)]
        for d in range(7):
            total = total + self.in1[d]
        self.acc[...] = total
        loop(1, 4, lambda d: self.copy2(d).start())

    def step3(self):
        w = self.w
        loop(1, 4, lambda d: self.copy2(d).wait_recv())
        total = self.acc[pl.ds(pl.multiple_of(w.x * 16, 16), 16)]
        for d in range(3):
            total = total + self.in2[d]
        self.in3[w.z] = total
        loop(1, 8, lambda d: self.copy3(d, w.z).start())

    def step4(self):
        w = self.w
        loop(1, 8, lambda d: self.copy3(d, (w.z - d + 8) % 8).wait_recv())
        total = self.in3[0]
        for d in range(1, 8):
            total = total + self.in3[d]
        self.g4[pl.ds(pl.multiple_of(w.x * 16, 16), 16)] = total
        loop(1, 4, lambda d: self.copy4(d, w.x).start())

    def step5(self):
        w = self.w
        loop(1, 4, lambda d: self.copy4(d, (w.x - d + 4) % 4).wait_recv())
        self.out[pl.ds(pl.multiple_of(w.r * 64, 64), 64)] = self.g4[...]
        loop(1, 8, lambda d: self.copy5(d, w.r).start())

    def finish(self):
        w = self.w
        loop(1, 8, lambda d: self.copy5(d, (w.r - d + 8) % 8).wait_recv())

    def drain(self):
        w = self.w
        loop(1, 8, lambda d: self.copy1(d).wait_send())
        loop(1, 4, lambda d: self.copy2(d).wait_send())
        loop(1, 8, lambda d: self.copy3(d, w.z).wait_send())
        loop(1, 4, lambda d: self.copy4(d, w.x).wait_send())
        loop(1, 8, lambda d: self.copy5(d, w.r).wait_send())


class Gather:
    def __init__(self, w, piece, rows, cols, sems):
        self.w = w
        self.piece = piece
        self.rows = rows
        self.cols = cols
        self.cs, self.cq, self.xs, self.xq, self.zs, self.zq = sems

    def col_copy(self, d, owner):
        w = self.w
        return rcopy(self.piece, self.cols.at[pl.ds(pl.multiple_of(owner * PIECE, PIECE), PIECE)],
                     self.cs.at[d - 1], self.cq.at[d - 1], (w.r + d) % 8, w.c)

    def x_copy(self, d, owner):
        w = self.w
        at = pl.multiple_of((w.z % 4) * BLOCK + owner * PIECE, PIECE)
        return rcopy(self.piece, self.rows.at[pl.ds(at, PIECE)], self.xs.at[d], self.xq.at[owner],
                     2 * w.x + w.z // 4, ((w.x + d) % 4) * 8 + w.z)

    def z_copy(self, way, t, half, at_z):
        w = self.w
        src_z = (at_z - t + 8) % 8 if way == 0 else (at_z + t) % 8
        rows = BLOCK // 2
        part = self.rows.at[pl.ds(pl.multiple_of((src_z % 4) * BLOCK + half * rows, rows), rows)]
        to = (w.z + 1) % 8 if way == 0 else (w.z + 7) % 8
        copy = rcopy(part, part, self.zs.at[way, t, half], self.zq.at[way, t, half], w.r, w.x * 8 + to)
        return copy, src_z // 4 == w.k

    def start(self):
        w = self.w
        for d in range(1, 4):
            self.x_copy(d, w.r).start()
        self_target = w.r == 2 * w.x + w.z // 4

        @pl.when(jnp.logical_not(self_target))
        def _():
            self.x_copy(0, w.r).start()

        @pl.when(self_target)
        def _():
            at = pl.multiple_of((w.z % 4) * BLOCK + w.r * PIECE, PIECE)
            self.rows[pl.ds(at, PIECE)] = self.piece[...]

        loop(1, 8, lambda d: self.col_copy(d, w.r).start())
        self.cols[pl.ds(pl.multiple_of(w.r * PIECE, PIECE), PIECE)] = self.piece[...]

    def wait_x(self):
        w = self.w

        @pl.when(w.z // 4 == w.k)
        def _():
            def one(owner):
                @pl.when(jnp.logical_not(jnp.logical_and(owner == w.r, w.x == w.y)))
                def _():
                    self.x_copy(0, owner).wait_recv()
            loop(0, 8, one)

    def halves(self, t):
        if t == 3:
            return ((0, 0), (1, 1))
        return ((0, 0), (1, 1), (0, 1), (1, 0))

    def step(self, t):
        z = self.w.z
        if t == 0:
            self.wait_x()
        for way, half in self.halves(max(t - 1, 0)):
            if t > 0:
                copy, mine = self.z_copy(way, t - 1, half, (z + 7) % 8 if way == 0 else (z + 1) % 8)

                @pl.when(mine)
                def _():
                    copy.wait_recv()
            if t < 4 and (way, half) in self.halves(t):
                copy, mine = self.z_copy(way, t, half, z)

                @pl.when(mine)
                def _():
                    copy.start()

    def wait_cols(self):
        w = self.w
        loop(1, 8, lambda d: self.col_copy(d, (w.r - d + 8) % 8).wait_recv())

    def drain(self):
        w = self.w
        for d in range(1, 4):
            self.x_copy(d, w.r).wait_send()

        @pl.when(w.r != 2 * w.x + w.z // 4)
        def _():
            self.x_copy(0, w.r).wait_send()

        loop(1, 8, lambda d: self.col_copy(d, w.r).wait_send())
        for t in range(4):
            for way, half in self.halves(t):
                copy, mine = self.z_copy(way, t, half, w.z)

                @pl.when(mine)
                def _():
                    copy.wait_send()


def invert(work, lo, hi):
    sub = lax.broadcasted_iota(jnp.int32, (8, NB), 0)
    lane = lax.broadcasted_iota(jnp.int32, (8, NB), 1)
    lanes = lax.broadcasted_iota(jnp.int32, (NB, NB), 1)
    both = range(2)

    def panel(p):
        at = pl.ds(pl.multiple_of(p * 8, 8), 8)
        rows = [work[m, at, :] for m in both]
        whole = [work[m] for m in both]
        for j in range(8):
            for m in both:
                column = jnp.broadcast_to(rows[m][:, j:j + 1], (8, NB))
                rest = jnp.where(lane == j, jnp.where(sub == j, 1.0, 0.0), rows[m])
                pivot = rest[j:j + 1, :] * (1.0 / column[j:j + 1, :])
                rows[m] = jnp.where(sub == j, pivot, rest - column * pivot)
        new = [jnp.where(lanes < 8, 0.0, whole[m]) for m in both]
        for j in range(8):
            for m in both:
                new[m] = new[m] - whole[m][:, j:j + 1] * rows[m][j:j + 1, :]
        for m in both:
            work[m] = pltpu.roll(new[m], NB - 8, 1)
            work[m, at, :] = pltpu.roll(rows[m], NB - 8, 1)
    loop(lo, hi, panel)


def barrier(w):
    sem = pltpu.get_barrier_semaphore()

    def greet(row, col):
        pl.semaphore_signal(sem, inc=1, device_id=(row, col), device_id_type=pl.DeviceIdType.MESH)

    loop(1, 8, lambda d: greet((w.r + d) % 8, w.c))
    loop(1, 8, lambda d: greet(w.r, w.x * 8 + (w.z + d) % 8))
    loop(1, 4, lambda d: greet(w.r, (w.x + d) % 4 * 8 + w.z))
    target = 2 * w.x + w.z // 4
    loop(1, 4, lambda d: greet(target, (w.x + d) % 4 * 8 + w.z))
    outside = w.r != target

    @pl.when(outside)
    def _():
        greet(target, w.c)

    receives = w.z // 4 == w.k

    @pl.when(receives)
    def _():
        def one(owner):
            @pl.when(jnp.logical_not(jnp.logical_and(owner == w.r, w.x == w.y)))
            def _():
                greet(owner, 8 * w.y + w.z)
        loop(0, 8, one)

    count = 20 + jnp.where(outside, 1, 0) + jnp.where(receives, jnp.where(w.x == w.y, 7, 8), 0)
    pl.semaphore_wait(sem, count)


def split(value):
    hi = value.astype(BF16)
    return hi, (value - hi.astype(F32)).astype(BF16)


def bdot(left, right, contract=((1,), (0,))):
    return lax.dot_general(left, right, (contract, ((), ())), preferred_element_type=F32)


def kernel(a_hbm, pan, out, a, piece_x, piece_y, rows_x, rows_y, cols_x, cols_y,
           gram, inner, yt, y, y_in, work, coef_x, coef_y, right1, right2, load_sem, store_sem, ys, yq, *rest):
    w = Where()
    n_ar = 16
    ar_g = AllReduce(w, gram, rest[:n_ar])
    ar_s = AllReduce(w, inner, rest[n_ar:2 * n_ar])
    sems = rest[2 * n_ar:]
    g_x = Gather(w, piece_x, rows_x, cols_x, sems[0:6])
    g_y = Gather(w, piece_y, rows_y, cols_y, sems[6:12])

    load = pltpu.make_async_copy(a_hbm, a, load_sem)
    load.start()
    v1 = pan[0]
    p2 = pan[1]
    piece_x[:, 0:NB] = v1.astype(BF16)
    piece_x[:, NB:] = p2.astype(BF16)
    barrier(w)
    g_x.start()
    both = jnp.concatenate([v1, p2], axis=1)
    gram[0:256] = fdot(both, v1, ((0,), (0,)))
    gram[256:512] = fdot(both, p2, ((0,), (0,)))
    ar_g.step1()
    yt[...] = jnp.zeros_like(yt)

    def product_block(b):
        def tile(i):
            at = pl.ds(pl.multiple_of(b * BLOCK + i * 256, 256), 256)
            yt[...] += bdot(rows_x[at], a[at], ((0,), (0,)))
        loop(0, BLOCK // 256, tile)

    def by_step(t, body):
        for way in range(2 if 0 < t < 4 else 1):
            src_z = (w.z - t + 8) % 8 if way == 0 else (w.z + t) % 8

            @pl.when(src_z // 4 == w.k)
            def _():
                body(src_z % 4)

    def product(t):
        by_step(t, product_block)

    g_x.step(0)
    ar_g.step2()
    load.wait()
    product(0)
    g_x.step(1)
    ar_g.step3()
    product(1)
    g_x.step(2)
    ar_g.step4()
    product(2)
    g_x.step(3)
    ar_g.step5()
    product(3)
    g_x.step(4)
    product(4)
    y[...] = yt[...].T.astype(BF16)

    def y_copy(d):
        to = (w.r + d) % 8
        return rcopy(y.at[pl.ds(pl.multiple_of(to * PIECE, PIECE), PIECE)], y_in.at[d - 1],
                     ys.at[d - 1], yq.at[d - 1], to, w.c)

    loop(1, 8, lambda d: y_copy(d).start())
    g_x.wait_cols()
    hi, lo = split(yt[...])
    s_t = bdot(hi, cols_x[...]) + bdot(lo, cols_x[...])
    inner[0:256] = s_t[:, 0:NB]
    inner[256:512] = s_t[:, NB:]
    ar_s.step1()

    ar_g.finish()
    cross = ar_g.out[256:384]
    eye = jnp.where(lax.broadcasted_iota(jnp.int32, (NB, NB), 0) == lax.broadcasted_iota(jnp.int32, (NB, NB), 1),
                    1.0, 0.0).astype(F32)
    work[0] = ar_g.out[0:128]
    work[1] = ar_g.out[384:512]
    invert(work, 0, 5)
    loop(1, 8, lambda d: y_copy(d).wait_recv())
    total = y[pl.ds(pl.multiple_of(w.r * PIECE, PIECE), PIECE)].astype(F32)
    for d in range(7):
        total = total + y_in[d].astype(F32)
    piece_y[...] = total.astype(BF16)
    g_y.start()
    ar_s.step2()
    invert(work, 5, 8)
    ar_s.step3()
    invert(work, 8, 11)
    g_y.step(0)
    invert(work, 11, 14)
    ar_s.step4()
    g_y.step(1)
    invert(work, 14, 16)
    f1 = 2.0 * work[0]
    f2 = 2.0 * work[1]
    mix = fdot(f1, cross)
    mix2 = fdot(cross, f2)
    ar_s.step5()
    g_y.step(2)
    ar_s.finish()
    s11 = ar_s.out[0:128]
    s21 = ar_s.out[128:256]
    s12 = ar_s.out[256:384]
    s22 = ar_s.out[384:512]
    tt = ((0,), (0,))
    b12 = s12 - fdot(s11, mix)
    b22 = s22 - fdot(s21, mix) - fdot(mix, b12, tt)
    l1 = 0.5 * fdot(f1, fdot(s11, f1, tt))
    h = fdot(f1, b12, tt) + fdot(l1, cross, tt)
    hc = fdot(h, cross, tt)
    l2 = 0.5 * fdot(f2, fdot(b22.T + hc + hc.T, f2))
    b = fdot(mix, l2) - (fdot(l1, mix2) + fdot(h, f2))
    zero = jnp.zeros((NB, NB), F32)
    for at, parts in ((coef_y, ((f1, zero), (zero, f2))), (coef_x, ((-l1, b, -mix), (zero, -l2, eye)))):
        for i, line in enumerate(parts):
            for j, part in enumerate(line):
                hi, lo = split(part)
                at[0, i * NB:(i + 1) * NB, j * NB:(j + 1) * NB] = hi
                at[1, i * NB:(i + 1) * NB, j * NB:(j + 1) * NB] = lo
    g_y.step(3)
    g_y.wait_cols()

    def form(x_ref, y_ref, at):
        xt = x_ref[at]
        yy = y_ref[at]
        both_x = bdot(xt, coef_x[0]) + bdot(xt, coef_x[1])
        wide = both_x[:, 0:2 * NB] + bdot(yy, coef_y[0]) + bdot(yy, coef_y[1])
        wb = wide.astype(BF16)
        return xt[:, 0:NB], wb[:, 0:NB], both_x[:, 2 * NB:].astype(BF16), wb[:, NB:]

    for i in range(BLOCK // 256):
        at = slice(i * 256, (i + 1) * 256)
        v1b, w1, v2, w2 = form(cols_x, cols_y, at)
        right1[0:NB, at] = w1.T
        right1[NB:, at] = v1b.T
        right2[0:NB, at] = w2.T
        right2[NB:, at] = v2.T

    def store(i):
        at = pl.ds(pl.multiple_of(i * 256, 256), 256)
        return pltpu.make_async_copy(a.at[at], out.at[at], store_sem.at[i])

    def update_block(block):
        for i in range(BLOCK // 256):
            at = pl.ds(pl.multiple_of(block * BLOCK + i * 256, 256), 256)
            v1b, w1, v2, w2 = form(rows_x, rows_y, at)
            left1 = jnp.concatenate([v1b, w1], axis=1)
            left2 = jnp.concatenate([v2, w2], axis=1)
            one = (a[at].astype(F32) - bdot(left1, right1[...])).astype(BF16)
            a[at] = (one.astype(F32) - bdot(left2, right2[...])).astype(BF16)
            store(block * (BLOCK // 256) + i).start()

    def update(t):
        by_step(t, update_block)

    for t in range(4):
        update(t)
    g_y.step(4)
    update(4)

    ar_g.drain()
    ar_s.drain()
    g_x.drain()
    g_y.drain()
    loop(1, 8, lambda d: y_copy(d).wait_send())
    loop(0, ROWS // 256, lambda i: store(i).wait())


def scratch():
    vm = pltpu.VMEM
    dma = pltpu.SemaphoreType.DMA
    shapes = [
        vm((ROWS, BLOCK), BF16),
        vm((PIECE, 256), BF16), vm((PIECE, 256), BF16),
        vm((ROWS, 256), BF16), vm((ROWS, 256), BF16),
        vm((BLOCK, 256), BF16), vm((BLOCK, 256), BF16),
        vm((512, 128), F32), vm((512, 128), F32),
        vm((256, BLOCK), F32), vm((BLOCK, 256), BF16), vm((7, PIECE, 256), BF16),
        vm((2, NB, NB), F32),
        vm((2, 2 * NB, 3 * NB), BF16), vm((2, 2 * NB, 2 * NB), BF16), vm((256, BLOCK), BF16), vm((256, BLOCK), BF16),
        dma(()), dma((ROWS // 256,)), dma((7,)), dma((7,)),
    ]
    for _ in range(2):
        shapes += [
            vm((7, 64, 128), F32), vm((64, 128), F32), vm((3, 16, 128), F32), vm((8, 16, 128), F32),
            vm((64, 128), F32), vm((512, 128), F32),
            dma((7,)), dma((7,)), dma((3,)), dma((3,)), dma((7,)), dma((7,)), dma((3,)), dma((3,)), dma((7,)), dma((7,)),
        ]
    for _ in range(2):
        shapes += [dma((7,)), dma((7,)), dma((4,)), dma((8,)), dma((2, 4, 2)), dma((2, 4, 2))]
    return shapes


def per_device(matrix, panels):
    return pl.pallas_call(
        kernel,
        out_shape=jax.ShapeDtypeStruct((ROWS, BLOCK), BF16),
        in_specs=[pl.BlockSpec(memory_space=pl.ANY), pl.BlockSpec(memory_space=pltpu.VMEM)],
        out_specs=pl.BlockSpec(memory_space=pl.ANY),
        scratch_shapes=scratch(),
        compiler_params=pltpu.CompilerParams(collective_id=0, has_side_effects=True, vmem_limit_bytes=48 * 1024 * 1024),
        cost_estimate=pl.CostEstimate(flops=3700000000, bytes_accessed=9437184, transcendentals=0),
    )(matrix, panels)


def solution(mesh):
    placed = (P("row", "col"), P(None, ("col", "row"), None))
    return jax.shard_map(
        per_device, mesh=mesh, in_specs=placed, out_specs=P("row", "col"), check_vma=False
    )
```

```python
import functools

import jax
import jax.numpy as jnp
from jax import lax
from jax.experimental import pallas as pl
from jax.experimental.pallas import tpu as pltpu
from jax.sharding import PartitionSpec as P

NB = 128
PIECE = 96
BLOCK = 768
ROWS = 3072
F32 = jnp.float32
BF16 = jnp.bfloat16


def fdot(left, right, contract=((1,), (0,))):
    return lax.dot_general(
        left, right, (contract, ((), ())), precision=lax.Precision.HIGHEST, preferred_element_type=F32
    )


def rcopy(src, dst, send, recv, row, col):
    return pltpu.make_async_remote_copy(
        src_ref=src, dst_ref=dst, send_sem=send, recv_sem=recv,
        device_id=(row, col), device_id_type=pl.DeviceIdType.MESH,
    )


class Where:
    def __init__(self):
        self.r = lax.axis_index("row")
        self.c = lax.axis_index("col")
        self.y = self.r // 2
        self.k = self.r % 2
        self.x = self.c // 8
        self.z = self.c % 8


def loop(lo, hi, body):
    def step(i, carry):
        body(i)
        return carry
    lax.fori_loop(lo, hi, step, 0)


class AllReduce:
    def __init__(self, w, src, refs):
        self.w = w
        self.src = src
        (self.in1, self.acc, self.in2, self.in3, self.g4, self.out,
         self.s1, self.q1, self.s2, self.q2, self.s3, self.q3, self.s4, self.q4, self.s5, self.q5) = refs

    def copy1(self, d):
        w = self.w
        to = (w.r + d) % 8
        return rcopy(self.src.at[pl.ds(pl.multiple_of(to * 64, 64), 64)], self.in1.at[d - 1],
                     self.s1.at[d - 1], self.q1.at[d - 1], to, w.c)

    def copy2(self, d):
        w = self.w
        to = (w.x + d) % 4
        return rcopy(self.acc.at[pl.ds(pl.multiple_of(to * 16, 16), 16)], self.in2.at[d - 1],
                     self.s2.at[d - 1], self.q2.at[d - 1], w.r, to * 8 + w.z)

    def copy3(self, d, slot):
        w = self.w
        to = (w.z + d) % 8
        return rcopy(self.in3.at[slot], self.in3.at[slot], self.s3.at[d - 1], self.q3.at[d - 1], w.r, w.x * 8 + to)

    def copy4(self, d, owner):
        w = self.w
        to = (w.x + d) % 4
        part = self.g4.at[pl.ds(pl.multiple_of(owner * 16, 16), 16)]
        return rcopy(part, part, self.s4.at[d - 1], self.q4.at[d - 1], w.r, to * 8 + w.z)

    def copy5(self, d, owner):
        w = self.w
        to = (w.r + d) % 8
        part = self.out.at[pl.ds(pl.multiple_of(owner * 64, 64), 64)]
        return rcopy(part, part, self.s5.at[d - 1], self.q5.at[d - 1], to, w.c)

    def step1(self):
        loop(1, 8, lambda d: self.copy1(d).start())

    def step2(self):
        loop(1, 8, lambda d: self.copy1(d).wait_recv())
        total = self.src[pl.ds(pl.multiple_of(self.w.r * 64, 64), 64)]
        for d in range(7):
            total = total + self.in1[d]
        self.acc[...] = total
        loop(1, 4, lambda d: self.copy2(d).start())

    def step3(self):
        w = self.w
        loop(1, 4, lambda d: self.copy2(d).wait_recv())
        total = self.acc[pl.ds(pl.multiple_of(w.x * 16, 16), 16)]
        for d in range(3):
            total = total + self.in2[d]
        self.in3[w.z] = total
        loop(1, 8, lambda d: self.copy3(d, w.z).start())

    def step4(self):
        w = self.w
        loop(1, 8, lambda d: self.copy3(d, (w.z - d + 8) % 8).wait_recv())
        total = self.in3[0]
        for d in range(1, 8):
            total = total + self.in3[d]
        self.g4[pl.ds(pl.multiple_of(w.x * 16, 16), 16)] = total
        loop(1, 4, lambda d: self.copy4(d, w.x).start())

    def step5(self):
        w = self.w
        loop(1, 4, lambda d: self.copy4(d, (w.x - d + 4) % 4).wait_recv())
        self.out[pl.ds(pl.multiple_of(w.r * 64, 64), 64)] = self.g4[...]
        loop(1, 8, lambda d: self.copy5(d, w.r).start())

    def finish(self):
        w = self.w
        loop(1, 8, lambda d: self.copy5(d, (w.r - d + 8) % 8).wait_recv())

    def drain(self):
        w = self.w
        loop(1, 8, lambda d: self.copy1(d).wait_send())
        loop(1, 4, lambda d: self.copy2(d).wait_send())
        loop(1, 8, lambda d: self.copy3(d, w.z).wait_send())
        loop(1, 4, lambda d: self.copy4(d, w.x).wait_send())
        loop(1, 8, lambda d: self.copy5(d, w.r).wait_send())


class Gather:
    def __init__(self, w, piece, rows, cols, sems):
        self.w = w
        self.piece = piece
        self.rows = rows
        self.cols = cols
        self.cs, self.cq, self.xs, self.xq, self.zs, self.zq = sems

    def col_copy(self, d, owner):
        w = self.w
        return rcopy(self.piece, self.cols.at[pl.ds(pl.multiple_of(owner * PIECE, PIECE), PIECE)],
                     self.cs.at[d - 1], self.cq.at[d - 1], (w.r + d) % 8, w.c)

    def x_copy(self, d, owner):
        w = self.w
        at = pl.multiple_of((w.z % 4) * BLOCK + owner * PIECE, PIECE)
        return rcopy(self.piece, self.rows.at[pl.ds(at, PIECE)], self.xs.at[d], self.xq.at[owner],
                     2 * w.x + w.z // 4, ((w.x + d) % 4) * 8 + w.z)

    def z_copy(self, way, t, half, at_z):
        w = self.w
        src_z = (at_z - t + 8) % 8 if way == 0 else (at_z + t) % 8
        rows = BLOCK // 2
        part = self.rows.at[pl.ds(pl.multiple_of((src_z % 4) * BLOCK + half * rows, rows), rows)]
        to = (w.z + 1) % 8 if way == 0 else (w.z + 7) % 8
        copy = rcopy(part, part, self.zs.at[way, t, half], self.zq.at[way, t, half], w.r, w.x * 8 + to)
        return copy, src_z // 4 == w.k

    def start(self):
        w = self.w
        for d in range(1, 4):
            self.x_copy(d, w.r).start()
        self_target = w.r == 2 * w.x + w.z // 4

        @pl.when(jnp.logical_not(self_target))
        def _():
            self.x_copy(0, w.r).start()

        @pl.when(self_target)
        def _():
            at = pl.multiple_of((w.z % 4) * BLOCK + w.r * PIECE, PIECE)
            self.rows[pl.ds(at, PIECE)] = self.piece[...]

    def start_cols(self):
        w = self.w
        loop(1, 8, lambda d: self.col_copy(d, w.r).start())
        self.cols[pl.ds(pl.multiple_of(w.r * PIECE, PIECE), PIECE)] = self.piece[...]

    def wait_x(self):
        w = self.w

        @pl.when(w.z // 4 == w.k)
        def _():
            def one(owner):
                @pl.when(jnp.logical_not(jnp.logical_and(owner == w.r, w.x == w.y)))
                def _():
                    self.x_copy(0, owner).wait_recv()
            loop(0, 8, one)

    def halves(self, t):
        if t == 3:
            return ((0, 0), (1, 1))
        return ((0, 0), (1, 1), (0, 1), (1, 0))

    def step(self, t):
        z = self.w.z
        if t == 0:
            self.wait_x()
        for way, half in self.halves(max(t - 1, 0)):
            if t > 0:
                copy, mine = self.z_copy(way, t - 1, half, (z + 7) % 8 if way == 0 else (z + 1) % 8)

                @pl.when(mine)
                def _():
                    copy.wait_recv()
            if t < 4 and (way, half) in self.halves(t):
                copy, mine = self.z_copy(way, t, half, z)

                @pl.when(mine)
                def _():
                    copy.start()

    def wait_cols(self):
        w = self.w
        loop(1, 8, lambda d: self.col_copy(d, (w.r - d + 8) % 8).wait_recv())

    def drain(self):
        w = self.w
        for d in range(1, 4):
            self.x_copy(d, w.r).wait_send()

        @pl.when(w.r != 2 * w.x + w.z // 4)
        def _():
            self.x_copy(0, w.r).wait_send()

        loop(1, 8, lambda d: self.col_copy(d, w.r).wait_send())
        for t in range(4):
            for way, half in self.halves(t):
                copy, mine = self.z_copy(way, t, half, w.z)

                @pl.when(mine)
                def _():
                    copy.wait_send()


def invert(work, lo, hi):
    sub = lax.broadcasted_iota(jnp.int32, (8, NB), 0)
    lane = lax.broadcasted_iota(jnp.int32, (8, NB), 1)
    lanes = lax.broadcasted_iota(jnp.int32, (NB, NB), 1)
    both = range(2)

    def panel(p):
        at = pl.ds(pl.multiple_of(p * 8, 8), 8)
        rows = [work[m, at, :] for m in both]
        whole = [work[m] for m in both]
        for j in range(8):
            for m in both:
                column = jnp.broadcast_to(rows[m][:, j:j + 1], (8, NB))
                rest = jnp.where(lane == j, jnp.where(sub == j, 1.0, 0.0), rows[m])
                pivot = rest[j:j + 1, :] * (1.0 / column[j:j + 1, :])
                rows[m] = jnp.where(sub == j, pivot, rest - column * pivot)
        new = [jnp.where(lanes < 8, 0.0, whole[m]) for m in both]
        for j in range(8):
            for m in both:
                new[m] = new[m] - whole[m][:, j:j + 1] * rows[m][j:j + 1, :]
        for m in both:
            work[m] = pltpu.roll(new[m], NB - 8, 1)
            work[m, at, :] = pltpu.roll(rows[m], NB - 8, 1)
    loop(lo, hi, panel)


def barrier(w):
    sem = pltpu.get_barrier_semaphore()

    def greet(row, col):
        pl.semaphore_signal(sem, inc=1, device_id=(row, col), device_id_type=pl.DeviceIdType.MESH)

    loop(1, 8, lambda d: greet((w.r + d) % 8, w.c))
    loop(1, 8, lambda d: greet(w.r, w.x * 8 + (w.z + d) % 8))
    loop(1, 4, lambda d: greet(w.r, (w.x + d) % 4 * 8 + w.z))
    target = 2 * w.x + w.z // 4
    loop(1, 4, lambda d: greet(target, (w.x + d) % 4 * 8 + w.z))
    outside = w.r != target

    @pl.when(outside)
    def _():
        greet(target, w.c)

    receives = w.z // 4 == w.k

    @pl.when(receives)
    def _():
        def one(owner):
            @pl.when(jnp.logical_not(jnp.logical_and(owner == w.r, w.x == w.y)))
            def _():
                greet(owner, 8 * w.y + w.z)
        loop(0, 8, one)

    count = 20 + jnp.where(outside, 1, 0) + jnp.where(receives, jnp.where(w.x == w.y, 7, 8), 0)
    pl.semaphore_wait(sem, count)


def split(value):
    hi = value.astype(BF16)
    return hi, (value - hi.astype(F32)).astype(BF16)


def bdot(left, right, contract=((1,), (0,))):
    return lax.dot_general(left, right, (contract, ((), ())), preferred_element_type=F32)


def kernel(a_hbm, pan, out, a, piece_x, piece_y, rows_x, rows_y, cols_x, cols_y,
           gram, inner, yt, y, y_in, work, coef_x, coef_y, right1, right2, left, load_sem, store_sem, ys, yq, *rest):
    w = Where()
    n_ar = 16
    ar_g = AllReduce(w, gram, rest[:n_ar])
    ar_s = AllReduce(w, inner, rest[n_ar:2 * n_ar])
    sems = rest[2 * n_ar:]
    g_x = Gather(w, piece_x, rows_x, cols_x, sems[0:6])
    g_y = Gather(w, piece_y, rows_y, cols_y, sems[6:12])

    load = pltpu.make_async_copy(a_hbm, a, load_sem)
    load.start()
    v1 = pan[0]
    p2 = pan[1]
    piece_x[:, 0:NB] = v1.astype(BF16)
    piece_x[:, NB:] = p2.astype(BF16)
    barrier(w)
    g_x.start()
    both = jnp.concatenate([v1, p2], axis=1)
    gram[0:256] = fdot(both, v1, ((0,), (0,)))
    gram[256:512] = fdot(both, p2, ((0,), (0,)))
    ar_g.step1()
    yt[...] = jnp.zeros_like(yt)

    def product_block(b):
        def tile(i):
            at = pl.ds(pl.multiple_of(b * BLOCK + i * 256, 256), 256)
            yt[...] += bdot(rows_x[at], a[at], ((0,), (0,)))
        loop(0, BLOCK // 256, tile)

    def by_step(t, body):
        for way in range(2 if 0 < t < 4 else 1):
            src_z = (w.z - t + 8) % 8 if way == 0 else (w.z + t) % 8

            @pl.when(src_z // 4 == w.k)
            def _():
                body(src_z % 4)

    def product(t):
        by_step(t, product_block)

    g_x.step(0)
    g_x.start_cols()
    ar_g.step2()
    load.wait()
    product(0)
    g_x.step(1)
    ar_g.step3()
    product(1)
    g_x.step(2)
    ar_g.step4()
    product(2)
    g_x.step(3)
    ar_g.step5()
    product(3)
    g_x.step(4)
    product(4)
    y[...] = yt[...].T.astype(BF16)

    def y_copy(d):
        to = (w.r + d) % 8
        return rcopy(y.at[pl.ds(pl.multiple_of(to * PIECE, PIECE), PIECE)], y_in.at[d - 1],
                     ys.at[d - 1], yq.at[d - 1], to, w.c)

    loop(1, 8, lambda d: y_copy(d).start())
    g_x.wait_cols()
    hi, lo = split(yt[...])
    s_t = bdot(hi, cols_x[...]) + bdot(lo, cols_x[...])
    inner[0:256] = s_t[:, 0:NB]
    inner[256:512] = s_t[:, NB:]
    ar_s.step1()

    ar_g.finish()
    cross = ar_g.out[256:384]
    eye = jnp.where(lax.broadcasted_iota(jnp.int32, (NB, NB), 0) == lax.broadcasted_iota(jnp.int32, (NB, NB), 1),
                    1.0, 0.0).astype(F32)
    work[0] = ar_g.out[0:128]
    work[1] = ar_g.out[384:512]
    invert(work, 0, 5)
    loop(1, 8, lambda d: y_copy(d).wait_recv())
    total = y[pl.ds(pl.multiple_of(w.r * PIECE, PIECE), PIECE)].astype(F32)
    for d in range(7):
        total = total + y_in[d].astype(F32)
    piece_y[...] = total.astype(BF16)
    g_y.start()
    ar_s.step2()
    invert(work, 5, 8)
    ar_s.step3()
    invert(work, 8, 11)
    g_y.step(0)
    g_y.start_cols()
    invert(work, 11, 14)
    ar_s.step4()
    g_y.step(1)
    invert(work, 14, 16)
    f1 = 2.0 * work[0]
    f2 = 2.0 * work[1]
    mix = fdot(f1, cross)
    mix2 = fdot(cross, f2)
    ar_s.step5()
    g_y.step(2)
    ar_s.finish()
    s11 = ar_s.out[0:128]
    s21 = ar_s.out[128:256]
    s12 = ar_s.out[256:384]
    s22 = ar_s.out[384:512]
    tt = ((0,), (0,))
    b12 = s12 - fdot(s11, mix)
    b22 = s22 - fdot(s21, mix) - fdot(mix, b12, tt)
    l1 = 0.5 * fdot(f1, fdot(s11, f1, tt))
    h = fdot(f1, b12, tt) + fdot(l1, cross, tt)
    hc = fdot(h, cross, tt)
    l2 = 0.5 * fdot(f2, fdot(b22.T + hc + hc.T, f2))
    b = fdot(mix, l2) - (fdot(l1, mix2) + fdot(h, f2))
    zero = jnp.zeros((NB, NB), F32)
    for i, line in enumerate(((f1, zero), (zero, f2))):
        for j, part in enumerate(line):
            hi, lo = split(part)
            coef_y[0, i * NB:(i + 1) * NB, j * NB:(j + 1) * NB] = hi
            coef_y[1, i * NB:(i + 1) * NB, j * NB:(j + 1) * NB] = lo
    for i, line in enumerate(((-l1, b, -mix), (zero, -l2, eye))):
        for j, part in enumerate(line):
            coef_x[i * NB:(i + 1) * NB, j * NB:(j + 1) * NB] = part.astype(BF16)
    g_y.step(3)
    g_y.wait_cols()

    def form(x_ref, y_ref, at):
        xt = x_ref[at]
        yy = y_ref[at]
        both_x = bdot(xt, coef_x[...])
        wide = both_x[:, 0:2 * NB] + bdot(yy, coef_y[0]) + bdot(yy, coef_y[1])
        wb = wide.astype(BF16)
        return xt[:, 0:NB], wb[:, 0:NB], both_x[:, 2 * NB:].astype(BF16), wb[:, NB:]

    v1b, w1, v2, w2 = form(cols_x, cols_y, slice(0, BLOCK))
    right1[0:NB] = w1.T
    right1[NB:] = v1b.T
    right2[0:NB] = w2.T
    right2[NB:] = v2.T

    def store(i):
        at = pl.ds(pl.multiple_of(i * BLOCK, BLOCK), BLOCK)
        return pltpu.make_async_copy(a.at[at], out.at[at], store_sem.at[i])

    def update_block(block):
        at = pl.ds(pl.multiple_of(block * BLOCK, BLOCK), BLOCK)
        v1b, w1, v2, w2 = form(rows_x, rows_y, at)
        left[0, :, 0:NB] = v1b
        left[0, :, NB:] = w1
        left[1, :, 0:NB] = v2
        left[1, :, NB:] = w2
        for n in range(BLOCK // 256):
            cut = slice(n * 256, (n + 1) * 256)
            one = (a[at, cut].astype(F32) - bdot(left[0], right1[:, cut])).astype(BF16)
            a[at, cut] = (one.astype(F32) - bdot(left[1], right2[:, cut])).astype(BF16)
        store(block).start()

    def update(t):
        by_step(t, update_block)

    for t in range(4):
        update(t)
    g_y.step(4)
    update(4)

    ar_g.drain()
    ar_s.drain()
    g_x.drain()
    g_y.drain()
    loop(1, 8, lambda d: y_copy(d).wait_send())
    loop(0, ROWS // BLOCK, lambda i: store(i).wait())


def scratch():
    vm = pltpu.VMEM
    dma = pltpu.SemaphoreType.DMA
    shapes = [
        vm((ROWS, BLOCK), BF16),
        vm((PIECE, 256), BF16), vm((PIECE, 256), BF16),
        vm((ROWS, 256), BF16), vm((ROWS, 256), BF16),
        vm((BLOCK, 256), BF16), vm((BLOCK, 256), BF16),
        vm((512, 128), F32), vm((512, 128), F32),
        vm((256, BLOCK), F32), vm((BLOCK, 256), BF16), vm((7, PIECE, 256), BF16),
        vm((2, NB, NB), F32),
        vm((2 * NB, 3 * NB), BF16), vm((2, 2 * NB, 2 * NB), BF16), vm((256, BLOCK), BF16), vm((256, BLOCK), BF16),
        vm((2, BLOCK, 256), BF16),
        dma(()), dma((ROWS // BLOCK,)), dma((7,)), dma((7,)),
    ]
    for _ in range(2):
        shapes += [
            vm((7, 64, 128), F32), vm((64, 128), F32), vm((3, 16, 128), F32), vm((8, 16, 128), F32),
            vm((64, 128), F32), vm((512, 128), F32),
            dma((7,)), dma((7,)), dma((3,)), dma((3,)), dma((7,)), dma((7,)), dma((3,)), dma((3,)), dma((7,)), dma((7,)),
        ]
    for _ in range(2):
        shapes += [dma((7,)), dma((7,)), dma((4,)), dma((8,)), dma((2, 4, 2)), dma((2, 4, 2))]
    return shapes


def per_device(matrix, panels):
    return pl.pallas_call(
        kernel,
        out_shape=jax.ShapeDtypeStruct((ROWS, BLOCK), BF16),
        in_specs=[pl.BlockSpec(memory_space=pl.ANY), pl.BlockSpec(memory_space=pltpu.VMEM)],
        out_specs=pl.BlockSpec(memory_space=pl.ANY),
        scratch_shapes=scratch(),
        compiler_params=pltpu.CompilerParams(collective_id=0, has_side_effects=True, vmem_limit_bytes=48 * 1024 * 1024),
        cost_estimate=pl.CostEstimate(flops=3700000000, bytes_accessed=9437184, transcendentals=0),
    )(matrix, panels)


def solution(mesh):
    placed = (P("row", "col"), P(None, ("col", "row"), None))
    return jax.shard_map(
        per_device, mesh=mesh, in_specs=placed, out_specs=P("row", "col"), check_vma=False
    )
```

```python
import functools

import jax
import jax.numpy as jnp
from jax import lax
from jax.experimental import pallas as pl
from jax.experimental.pallas import tpu as pltpu
from jax.sharding import PartitionSpec as P

NB = 128
PIECE = 96
BLOCK = 768
ROWS = 3072
F32 = jnp.float32
BF16 = jnp.bfloat16


def fdot(left, right, contract=((1,), (0,))):
    return lax.dot_general(
        left, right, (contract, ((), ())), precision=lax.Precision.HIGHEST, preferred_element_type=F32
    )


def rcopy(src, dst, send, recv, row, col):
    return pltpu.make_async_remote_copy(
        src_ref=src, dst_ref=dst, send_sem=send, recv_sem=recv,
        device_id=(row, col), device_id_type=pl.DeviceIdType.MESH,
    )


class Where:
    def __init__(self):
        self.r = lax.axis_index("row")
        self.c = lax.axis_index("col")
        self.y = self.r // 2
        self.k = self.r % 2
        self.x = self.c // 8
        self.z = self.c % 8
        self.target = 2 * self.x + self.z // 4
        self.outside = self.r != self.target

    def by_step(self, t, body):
        for way in range(2 if 0 < t < 4 else 1):
            src_z = (self.z - t + 8) % 8 if way == 0 else (self.z + t) % 8

            @pl.when(src_z // 4 == self.k)
            def _():
                body(src_z % 4)


def loop(lo, hi, body):
    def step(i, carry):
        body(i)
        return carry
    lax.fori_loop(lo, hi, step, 0)


class AllReduce:
    def __init__(self, w, src, refs):
        self.w = w
        self.src = src
        (self.in1, self.acc, self.in2, self.in3, self.g4, self.out,
         self.s1, self.q1, self.s2, self.q2, self.s3, self.q3, self.s4, self.q4, self.s5, self.q5) = refs

    def copy1(self, d):
        w = self.w
        to = (w.r + d) % 8
        return rcopy(self.src.at[pl.ds(pl.multiple_of(to * 64, 64), 64)], self.in1.at[d - 1],
                     self.s1.at[d - 1], self.q1.at[d - 1], to, w.c)

    def copy2(self, d):
        w = self.w
        to = (w.x + d) % 4
        return rcopy(self.acc.at[pl.ds(pl.multiple_of(to * 16, 16), 16)], self.in2.at[d - 1],
                     self.s2.at[d - 1], self.q2.at[d - 1], w.r, to * 8 + w.z)

    def copy3(self, d, slot):
        w = self.w
        to = (w.z + d) % 8
        return rcopy(self.in3.at[slot], self.in3.at[slot], self.s3.at[d - 1], self.q3.at[d - 1], w.r, w.x * 8 + to)

    def copy4(self, d, owner):
        w = self.w
        to = (w.x + d) % 4
        part = self.g4.at[pl.ds(pl.multiple_of(owner * 16, 16), 16)]
        return rcopy(part, part, self.s4.at[d - 1], self.q4.at[d - 1], w.r, to * 8 + w.z)

    def copy5(self, d, owner):
        w = self.w
        to = (w.r + d) % 8
        part = self.out.at[pl.ds(pl.multiple_of(owner * 64, 64), 64)]
        return rcopy(part, part, self.s5.at[d - 1], self.q5.at[d - 1], to, w.c)

    def step1(self):
        loop(1, 8, lambda d: self.copy1(d).start())

    def step2(self):
        loop(1, 8, lambda d: self.copy1(d).wait_recv())
        total = self.src[pl.ds(pl.multiple_of(self.w.r * 64, 64), 64)]
        for d in range(7):
            total = total + self.in1[d]
        self.acc[...] = total
        loop(1, 4, lambda d: self.copy2(d).start())

    def step3(self):
        w = self.w
        loop(1, 4, lambda d: self.copy2(d).wait_recv())
        total = self.acc[pl.ds(pl.multiple_of(w.x * 16, 16), 16)]
        for d in range(3):
            total = total + self.in2[d]
        self.in3[w.z] = total
        loop(1, 8, lambda d: self.copy3(d, w.z).start())

    def step4(self):
        w = self.w
        loop(1, 8, lambda d: self.copy3(d, (w.z - d + 8) % 8).wait_recv())
        total = self.in3[0]
        for d in range(1, 8):
            total = total + self.in3[d]
        self.g4[pl.ds(pl.multiple_of(w.x * 16, 16), 16)] = total
        loop(1, 4, lambda d: self.copy4(d, w.x).start())

    def step5(self):
        w = self.w
        loop(1, 4, lambda d: self.copy4(d, (w.x - d + 4) % 4).wait_recv())
        self.out[pl.ds(pl.multiple_of(w.r * 64, 64), 64)] = self.g4[...]
        loop(1, 8, lambda d: self.copy5(d, w.r).start())

    def finish(self):
        w = self.w
        loop(1, 8, lambda d: self.copy5(d, (w.r - d + 8) % 8).wait_recv())

    def drain(self):
        w = self.w
        loop(1, 8, lambda d: self.copy1(d).wait_send())
        loop(1, 4, lambda d: self.copy2(d).wait_send())
        loop(1, 8, lambda d: self.copy3(d, w.z).wait_send())
        loop(1, 4, lambda d: self.copy4(d, w.x).wait_send())
        loop(1, 8, lambda d: self.copy5(d, w.r).wait_send())


class Gather:
    def __init__(self, w, piece, rows, cols, sems):
        self.w = w
        self.piece = piece
        self.rows = rows
        self.cols = cols
        self.cs, self.cq, self.xs, self.xq, self.zs, self.zq, self.ts, self.tq, self.qs, self.qq, self.es, self.eq = sems

    def col_copy(self, d, owner):
        w = self.w
        return rcopy(self.piece, self.cols.at[:, pl.ds(pl.multiple_of(owner * PIECE, PIECE), PIECE)],
                     self.cs.at[d - 1], self.cq.at[d - 1], (w.r + d) % 8, w.c)

    def x_copy(self, d, owner):
        w = self.w
        at = pl.multiple_of((w.z % 4) * BLOCK + owner * PIECE, PIECE)
        return rcopy(self.piece.at[0], self.rows.at[0, pl.ds(at, PIECE)], self.xs.at[d], self.xq.at[owner],
                     w.target, ((w.x + d) % 4) * 8 + w.z)

    def turn_copy(self, owner):
        w = self.w
        at = pl.multiple_of((w.z % 4) * BLOCK + owner * PIECE, PIECE)
        return rcopy(self.piece.at[1], self.rows.at[1, pl.ds(at, PIECE)], self.ts, self.tq.at[owner % 2],
                     w.target, 8 * w.y + w.z)

    def quarter_copy(self, way, t, at_z):
        w = self.w
        src_z = (at_z - t + 8) % 8 if way == 0 else (at_z + t) % 8
        base = (src_z % 4) * BLOCK + w.x * 2 * PIECE
        if t < 3:
            part = self.rows.at[1, pl.ds(pl.multiple_of(base, 2 * PIECE), 2 * PIECE)]
        else:
            part = self.rows.at[1, pl.ds(pl.multiple_of(base + way * PIECE, PIECE), PIECE)]
        to = (w.z + 1) % 8 if way == 0 else (w.z + 7) % 8
        copy = rcopy(part, part, self.qs.at[way, t], self.qq.at[way, t], w.r, w.x * 8 + to)
        return copy, src_z // 4 == w.k

    def exchange_copy(self, d, block, owner_x):
        w = self.w
        at = pl.multiple_of(block * BLOCK + owner_x * 2 * PIECE, 2 * PIECE)
        part = self.rows.at[1, pl.ds(at, 2 * PIECE)]
        at = block * 3 + d - 1
        return rcopy(part, part, self.es.at[at], self.eq.at[at], w.r, ((w.x + d) % 4) * 8 + w.z)

    def quarter_step(self, t):
        w = self.w
        z = w.z
        if t == 0:
            @pl.when(z // 4 == w.k)
            def _():
                for kk in range(2):
                    @pl.when(jnp.logical_not(jnp.logical_and(w.x == w.y, w.k == kk)))
                    def _():
                        self.turn_copy(2 * w.x + kk).wait_recv()
        for way in range(2):
            if t > 0:
                copy, mine = self.quarter_copy(way, t - 1, (z + 7) % 8 if way == 0 else (z + 1) % 8)

                @pl.when(mine)
                def _():
                    copy.wait_recv()
            if t < 4:
                copy, mine = self.quarter_copy(way, t, z)

                @pl.when(mine)
                def _():
                    copy.start()
        w.by_step(t, lambda block: loop(1, 4, lambda d: self.exchange_copy(d, block, w.x).start()))

    def wait_exchange(self, t):
        w = self.w
        w.by_step(t, lambda block: loop(1, 4, lambda d: self.exchange_copy(d, block, (w.x - d + 4) % 4).wait_recv()))

    def z_copy(self, way, t, half, at_z):
        w = self.w
        src_z = (at_z - t + 8) % 8 if way == 0 else (at_z + t) % 8
        rows = BLOCK // 2
        part = self.rows.at[0, pl.ds(pl.multiple_of((src_z % 4) * BLOCK + half * rows, rows), rows)]
        to = (w.z + 1) % 8 if way == 0 else (w.z + 7) % 8
        copy = rcopy(part, part, self.zs.at[way, t, half], self.zq.at[way, t, half], w.r, w.x * 8 + to)
        return copy, src_z // 4 == w.k

    def start(self):
        w = self.w
        loop(1, 4, lambda d: self.x_copy(d, w.r).start())

        @pl.when(w.outside)
        def _():
            self.x_copy(0, w.r).start()
            self.turn_copy(w.r).start()

        @pl.when(jnp.logical_not(w.outside))
        def _():
            at = pl.multiple_of((w.z % 4) * BLOCK + w.r * PIECE, PIECE)
            self.rows[:, pl.ds(at, PIECE)] = self.piece[...]

    def start_cols(self):
        w = self.w
        loop(1, 8, lambda d: self.col_copy(d, w.r).start())
        self.cols[:, pl.ds(pl.multiple_of(w.r * PIECE, PIECE), PIECE)] = self.piece[...]

    def wait_x(self):
        w = self.w

        @pl.when(w.z // 4 == w.k)
        def _():
            def one(owner):
                @pl.when(jnp.logical_not(jnp.logical_and(owner == w.r, w.x == w.y)))
                def _():
                    self.x_copy(0, owner).wait_recv()
            loop(0, 8, one)

    def halves(self, t):
        if t == 3:
            return ((0, 0), (1, 1))
        return ((0, 0), (1, 1), (0, 1), (1, 0))

    def step(self, t):
        z = self.w.z
        if t == 0:
            self.wait_x()
        for way, half in self.halves(max(t - 1, 0)):
            if t > 0:
                copy, mine = self.z_copy(way, t - 1, half, (z + 7) % 8 if way == 0 else (z + 1) % 8)

                @pl.when(mine)
                def _():
                    copy.wait_recv()
            if t < 4 and (way, half) in self.halves(t):
                copy, mine = self.z_copy(way, t, half, z)

                @pl.when(mine)
                def _():
                    copy.start()
        self.quarter_step(t)

    def wait_cols(self):
        w = self.w
        loop(1, 8, lambda d: self.col_copy(d, (w.r - d + 8) % 8).wait_recv())

    def drain(self):
        w = self.w
        loop(1, 4, lambda d: self.x_copy(d, w.r).wait_send())

        @pl.when(w.outside)
        def _():
            self.x_copy(0, w.r).wait_send()
            self.turn_copy(w.r).wait_send()

        def sent(block):
            loop(1, 4, lambda d: self.exchange_copy(d, block, w.x).wait_send())
        loop(0, 4, sent)
        loop(1, 8, lambda d: self.col_copy(d, w.r).wait_send())
        for t in range(4):
            for way in range(2):
                copy, mine = self.quarter_copy(way, t, w.z)

                @pl.when(mine)
                def _():
                    copy.wait_send()
            for way, half in self.halves(t):
                copy, mine = self.z_copy(way, t, half, w.z)

                @pl.when(mine)
                def _():
                    copy.wait_send()


def invert(work, lo, hi):
    sub = lax.broadcasted_iota(jnp.int32, (8, NB), 0)
    lane = lax.broadcasted_iota(jnp.int32, (8, NB), 1)
    lanes = lax.broadcasted_iota(jnp.int32, (NB, NB), 1)
    both = range(2)

    def panel(p):
        at = pl.ds(pl.multiple_of(p * 8, 8), 8)
        rows = [work[m, at, :] for m in both]
        whole = [work[m] for m in both]
        for j in range(8):
            for m in both:
                column = jnp.broadcast_to(rows[m][:, j:j + 1], (8, NB))
                rest = jnp.where(lane == j, jnp.where(sub == j, 1.0, 0.0), rows[m])
                pivot = rest[j:j + 1, :] * (1.0 / column[j:j + 1, :])
                rows[m] = jnp.where(sub == j, pivot, rest - column * pivot)
        new = [jnp.where(lanes < 8, 0.0, whole[m]) for m in both]
        for j in range(8):
            for m in both:
                new[m] = new[m] - whole[m][:, j:j + 1] * rows[m][j:j + 1, :]
        for m in both:
            work[m] = pltpu.roll(new[m], NB - 8, 1)
            work[m, at, :] = pltpu.roll(rows[m], NB - 8, 1)
    loop(lo, hi, panel)


def barrier(w):
    sem = pltpu.get_barrier_semaphore()

    def greet(row, col):
        pl.semaphore_signal(sem, inc=1, device_id=(row, col), device_id_type=pl.DeviceIdType.MESH)

    loop(1, 8, lambda d: greet((w.r + d) % 8, w.c))
    loop(1, 8, lambda d: greet(w.r, w.x * 8 + (w.z + d) % 8))
    loop(1, 4, lambda d: greet(w.r, (w.x + d) % 4 * 8 + w.z))
    loop(1, 4, lambda d: greet(w.target, (w.x + d) % 4 * 8 + w.z))

    @pl.when(w.outside)
    def _():
        greet(w.target, w.c)
        greet(w.target, w.y * 8 + w.z)

    receives = w.z // 4 == w.k

    @pl.when(receives)
    def _():
        def one(owner):
            @pl.when(jnp.logical_not(jnp.logical_and(owner == w.r, w.x == w.y)))
            def _():
                greet(owner, 8 * w.y + w.z)
        loop(0, 8, one)

    @pl.when(receives)
    def _():
        for kk in range(2):
            @pl.when(jnp.logical_not(jnp.logical_and(w.x == w.y, w.k == kk)))
            def _():
                greet(2 * w.x + kk, 8 * w.y + w.z)

    count = 20 + jnp.where(w.outside, 2, 0) + jnp.where(receives, jnp.where(w.x == w.y, 8, 10), 0)
    pl.semaphore_wait(sem, count)


def split(value):
    hi = value.astype(BF16)
    return hi, (value - hi.astype(F32)).astype(BF16)


def bdot(left, right, contract=((1,), (0,))):
    return lax.dot_general(left, right, (contract, ((), ())), preferred_element_type=F32)


def pair(ref, at):
    return jnp.concatenate([ref[0, at], ref[1, at]], axis=1)


def kernel(a_hbm, pan, out, a, piece_x, piece_y, rows_x, rows_y, cols_x, cols_y,
           gram, inner, yt, y, y_in, work, coef_x, coef_y, right1, right2, left, load_sem, store_sem, ys, yq, *rest):
    w = Where()
    n_ar = 16
    ar_g = AllReduce(w, gram, rest[:n_ar])
    ar_s = AllReduce(w, inner, rest[n_ar:2 * n_ar])
    sems = rest[2 * n_ar:]
    g_x = Gather(w, piece_x, rows_x, cols_x, sems[0:12])
    g_y = Gather(w, piece_y, rows_y, cols_y, sems[12:24])

    load = pltpu.make_async_copy(a_hbm, a, load_sem)
    load.start()
    v1 = pan[0]
    p2 = pan[1]
    piece_x[0] = v1.astype(BF16)
    piece_x[1] = p2.astype(BF16)
    barrier(w)
    g_x.start()
    both = jnp.concatenate([v1, p2], axis=1)
    gram[0:256] = fdot(both, v1, ((0,), (0,)))
    gram[256:512] = fdot(both, p2, ((0,), (0,)))
    ar_g.step1()
    yt[...] = jnp.zeros_like(yt)

    def product_block(b):
        def tile(i):
            at = pl.ds(pl.multiple_of(b * BLOCK + i * 256, 256), 256)
            yt[...] += bdot(pair(rows_x, at), a[at], ((0,), (0,)))
        loop(0, BLOCK // 256, tile)

    def product(t):
        g_x.wait_exchange(t)
        w.by_step(t, product_block)

    g_x.step(0)
    g_x.start_cols()
    ar_g.step2()
    load.wait()
    product(0)
    g_x.step(1)
    ar_g.step3()
    product(1)
    g_x.step(2)
    ar_g.step4()
    product(2)
    g_x.step(3)
    ar_g.step5()
    product(3)
    g_x.step(4)
    product(4)
    y[...] = yt[...].T.astype(BF16)

    def y_copy(d):
        to = (w.r + d) % 8
        return rcopy(y.at[pl.ds(pl.multiple_of(to * PIECE, PIECE), PIECE)], y_in.at[d - 1],
                     ys.at[d - 1], yq.at[d - 1], to, w.c)

    loop(1, 8, lambda d: y_copy(d).start())
    g_x.wait_cols()
    hi, lo = split(yt[...])
    col_x = pair(cols_x, slice(0, BLOCK))
    s_t = bdot(hi, col_x) + bdot(lo, col_x)
    inner[0:256] = s_t[:, 0:NB]
    inner[256:512] = s_t[:, NB:]
    ar_s.step1()

    ar_g.finish()
    cross = ar_g.out[256:384]
    eye = jnp.where(lax.broadcasted_iota(jnp.int32, (NB, NB), 0) == lax.broadcasted_iota(jnp.int32, (NB, NB), 1),
                    1.0, 0.0).astype(F32)
    work[0] = ar_g.out[0:128]
    work[1] = ar_g.out[384:512]
    invert(work, 0, 5)
    loop(1, 8, lambda d: y_copy(d).wait_recv())
    total = y[pl.ds(pl.multiple_of(w.r * PIECE, PIECE), PIECE)].astype(F32)
    for d in range(7):
        total = total + y_in[d].astype(F32)
    piece_y[0] = total[:, 0:NB].astype(BF16)
    piece_y[1] = total[:, NB:].astype(BF16)
    g_y.start()
    ar_s.step2()
    invert(work, 5, 8)
    ar_s.step3()
    invert(work, 8, 11)
    g_y.step(0)
    g_y.start_cols()
    invert(work, 11, 14)
    ar_s.step4()
    g_y.step(1)
    invert(work, 14, 16)
    f1 = 2.0 * work[0]
    f2 = 2.0 * work[1]
    mix = fdot(f1, cross)
    mix2 = fdot(cross, f2)
    ar_s.step5()
    g_y.step(2)
    ar_s.finish()
    s11 = ar_s.out[0:128]
    s21 = ar_s.out[128:256]
    s12 = ar_s.out[256:384]
    s22 = ar_s.out[384:512]
    tt = ((0,), (0,))
    b12 = s12 - fdot(s11, mix)
    b22 = s22 - fdot(s21, mix) - fdot(mix, b12, tt)
    l1 = 0.5 * fdot(f1, fdot(s11, f1, tt))
    h = fdot(f1, b12, tt) + fdot(l1, cross, tt)
    hc = fdot(h, cross, tt)
    l2 = 0.5 * fdot(f2, fdot(b22.T + hc + hc.T, f2))
    b = fdot(mix, l2) - (fdot(l1, mix2) + fdot(h, f2))
    zero = jnp.zeros((NB, NB), F32)
    for i, line in enumerate(((f1, zero), (zero, f2))):
        for j, part in enumerate(line):
            hi, lo = split(part)
            coef_y[0, i * NB:(i + 1) * NB, j * NB:(j + 1) * NB] = hi
            coef_y[1, i * NB:(i + 1) * NB, j * NB:(j + 1) * NB] = lo
    for i, line in enumerate(((-l1, b, -mix), (zero, -l2, eye))):
        for j, part in enumerate(line):
            coef_x[i * NB:(i + 1) * NB, j * NB:(j + 1) * NB] = part.astype(BF16)
    g_y.step(3)
    g_y.wait_cols()

    def form(x_ref, y_ref, at):
        xt = pair(x_ref, at)
        yy = pair(y_ref, at)
        both_x = bdot(xt, coef_x[...])
        wide = both_x[:, 0:2 * NB] + bdot(yy, coef_y[0]) + bdot(yy, coef_y[1])
        wb = wide.astype(BF16)
        return xt[:, 0:NB], wb[:, 0:NB], both_x[:, 2 * NB:].astype(BF16), wb[:, NB:]

    v1b, w1, v2, w2 = form(cols_x, cols_y, slice(0, BLOCK))
    right1[0:NB] = w1.T
    right1[NB:] = v1b.T
    right2[0:NB] = w2.T
    right2[NB:] = v2.T

    def store(i):
        at = pl.ds(pl.multiple_of(i * BLOCK, BLOCK), BLOCK)
        return pltpu.make_async_copy(a.at[at], out.at[at], store_sem.at[i])

    def update_block(block):
        at = pl.ds(pl.multiple_of(block * BLOCK, BLOCK), BLOCK)
        v1b, w1, v2, w2 = form(rows_x, rows_y, at)
        left[0, :, 0:NB] = v1b
        left[0, :, NB:] = w1
        left[1, :, 0:NB] = v2
        left[1, :, NB:] = w2
        for n in range(BLOCK // 256):
            cut = slice(n * 256, (n + 1) * 256)
            one = (a[at, cut].astype(F32) - bdot(left[0], right1[:, cut])).astype(BF16)
            a[at, cut] = (one.astype(F32) - bdot(left[1], right2[:, cut])).astype(BF16)
        store(block).start()

    def update(t):
        g_y.wait_exchange(t)
        w.by_step(t, update_block)

    for t in range(4):
        update(t)
    g_y.step(4)
    update(4)

    ar_g.drain()
    ar_s.drain()
    g_x.drain()
    g_y.drain()
    loop(1, 8, lambda d: y_copy(d).wait_send())
    loop(0, ROWS // BLOCK, lambda i: store(i).wait())


def scratch():
    vm = pltpu.VMEM
    dma = pltpu.SemaphoreType.DMA
    shapes = [
        vm((ROWS, BLOCK), BF16),
        vm((2, PIECE, NB), BF16), vm((2, PIECE, NB), BF16),
        vm((2, ROWS, NB), BF16), vm((2, ROWS, NB), BF16),
        vm((2, BLOCK, NB), BF16), vm((2, BLOCK, NB), BF16),
        vm((512, 128), F32), vm((512, 128), F32),
        vm((256, BLOCK), F32), vm((BLOCK, 256), BF16), vm((7, PIECE, 256), BF16),
        vm((2, NB, NB), F32),
        vm((2 * NB, 3 * NB), BF16), vm((2, 2 * NB, 2 * NB), BF16), vm((256, BLOCK), BF16), vm((256, BLOCK), BF16),
        vm((2, BLOCK, 256), BF16),
        dma(()), dma((ROWS // BLOCK,)), dma((7,)), dma((7,)),
    ]
    for _ in range(2):
        shapes += [
            vm((7, 64, 128), F32), vm((64, 128), F32), vm((3, 16, 128), F32), vm((8, 16, 128), F32),
            vm((64, 128), F32), vm((512, 128), F32),
            dma((7,)), dma((7,)), dma((3,)), dma((3,)), dma((7,)), dma((7,)), dma((3,)), dma((3,)), dma((7,)), dma((7,)),
        ]
    for _ in range(2):
        shapes += [dma((7,)), dma((7,)), dma((4,)), dma((8,)), dma((2, 4, 2)), dma((2, 4, 2)),
                   dma(()), dma((2,)), dma((2, 4)), dma((2, 4)), dma((12,)), dma((12,))]
    return shapes


def per_device(matrix, panels):
    return pl.pallas_call(
        kernel,
        out_shape=jax.ShapeDtypeStruct((ROWS, BLOCK), BF16),
        in_specs=[pl.BlockSpec(memory_space=pl.ANY), pl.BlockSpec(memory_space=pltpu.VMEM)],
        out_specs=pl.BlockSpec(memory_space=pl.ANY),
        scratch_shapes=scratch(),
        compiler_params=pltpu.CompilerParams(collective_id=0, has_side_effects=True, vmem_limit_bytes=48 * 1024 * 1024),
        cost_estimate=pl.CostEstimate(flops=3700000000, bytes_accessed=9437184, transcendentals=0),
    )(matrix, panels)


def solution(mesh):
    placed = (P("row", "col"), P(None, ("col", "row"), None))
    return jax.shard_map(
        per_device, mesh=mesh, in_specs=placed, out_specs=P("row", "col"), check_vma=False
    )
```
